32 devices in a mesh: groups: 2 (over y), row: 8 (over z, x), col: 2 (over core).
Axes of the slice: x: 2, y: 2, z: 4, core: 2. Of those that a mesh axis runs over, the one named last changes fastest.
Arguments:
- queries: float32 [128, 4096], P(('groups', 'row'), 'col'), parts along dimension 0, may hold values from -3 to 3
- documents: float32 [128, 4096], P(('groups', 'row'), 'col'), parts along dimension 0, may hold values from -3 to 3
- positive: int32 [128], P(('groups', 'row')), parts along dimension 0, may hold values from 0 to 63, as said below
- hard_ids: int32 [128, 7], P(('groups', 'row')), parts along dimension 0, may hold values from 0 to 63
Outputs:
- request_derivative: float32 [128, 4096], P(('groups', 'row'), 'col'), parts along dimension 0
- passage_derivative: float32 [128, 4096], P(('groups', 'row'), 'col'), parts along dimension 0
- loss_rows: float32 [128], P(('groups', 'row')), parts along dimension 0
The draws below stay inside these ranges and needn't reach their ends.
There are 2 independent parts, one for each index of `groups`. The reference program is written for one: setup_inputs(seed, part) draws one part's arguments, and reference() takes and returns one part's arrays. A program takes and returns all parts, laid end to end along the dimension named above; each array names one. Nothing has to cross between parts.
Inputs may be any that keep to these rules, and one draw needn't show every extreme that they name: positive[i] is a document of query i's own aligned block of 8, from i - i % 8 to i - i % 8 + 7; within each block every document is the positive of exactly one query.
All inputs are finite; a program needn't handle non-finite values.
Results may differ from the reference program's by a relative error of at most 0.006.
Values may be sent and summed in bfloat16 or wider, within the bound.
A program may use at most 64 MiB of HBM per device.

```python
import jax
import jax.numpy as jnp

LATENT_DIMENSION = 4096
ROWS = 8
HARD = 7
BATCH = 64


doc_level = 0.24


peak_level = 0.53


shared_level = 0.24


flat_noise = 0.08


def positive_table(key):
    blocks = BATCH // ROWS
    keys = jax.random.split(jax.random.fold_in(key, 11), blocks)
    orders = jax.vmap(lambda single: jax.random.permutation(single, ROWS))(keys)
    starts = jnp.arange(blocks, dtype=jnp.int32)[:, None] * ROWS
    return (orders.astype(jnp.int32) + starts).reshape(BATCH)


def doc_table(key):
    width_scale = LATENT_DIMENSION ** (-0.25)
    doc_sigma = doc_level * width_scale
    base = jnp.clip(jax.random.normal(jax.random.fold_in(key, 21), (BATCH, LATENT_DIMENSION), jnp.float32), -5.0, 5.0) * doc_sigma
    return base


def draw_documents(key, part):
    return doc_table(key)


def draw_positive(key, part):
    return positive_table(key)


def draw_queries(key, part):
    width_scale = LATENT_DIMENSION ** (-0.25)
    peaked = jnp.clip(jax.random.normal(jax.random.fold_in(key, 31), (BATCH, LATENT_DIMENSION), jnp.float32), -4.0, 4.0) * (peak_level * width_scale)
    shared = jnp.clip(jax.random.normal(jax.random.fold_in(key, 34), (1, LATENT_DIMENSION), jnp.float32), -4.0, 4.0) * (shared_level * width_scale)
    jitter = jnp.clip(jax.random.normal(jax.random.fold_in(key, 35), (BATCH, LATENT_DIMENSION), jnp.float32), -4.0, 4.0) * (flat_noise * width_scale)
    flat = shared + jitter
    flat_rows = jax.random.bernoulli(jax.random.fold_in(key, 36), 0.5, (BATCH, 1))
    return jnp.where(flat_rows, flat, peaked)


def with_ends(values, rng, least, top_value):
    extent = values.shape
    index_at = [jax.random.randint(jax.random.fold_in(rng, axis), (), 0, extent[axis]) for axis in range(len(extent))]
    values = values.at[tuple(index_at)].set(least)
    longest = extent.index(max(extent))
    index_at[longest] = (index_at[longest] + 1) % extent[longest]
    return values.at[tuple(index_at)].set(top_value)


def setup_inputs(seed: int = 0, part: int = 0) -> dict:
    splits = jax.random.split(jax.random.key(seed), 5)
    part_keys = jax.random.split(jax.random.fold_in(splits[4], part), 5)
    queries = draw_queries(jax.random.fold_in(jax.random.fold_in(splits[4], part), 71), part)
    documents = draw_documents(jax.random.fold_in(jax.random.fold_in(splits[4], part), 71), part)
    positive = draw_positive(jax.random.fold_in(jax.random.fold_in(splits[4], part), 71), part)
    hard_ids = with_ends(jax.random.randint(part_keys[3], (BATCH, HARD), 0, BATCH), jax.random.fold_in(part_keys[3], 1), 0, BATCH - 1).astype(jnp.int32)
    return dict(queries=queries, documents=documents, positive=positive, hard_ids=hard_ids)


sharpness_divisor = 0.05
hardness_multiplier = 3.0


def weigh(request_similarity, passage_similarity, positive, hard_ids, batch_size):
    columns = jnp.arange(batch_size, dtype=jnp.int32)
    hardness_tally = jnp.zeros(request_similarity.shape, jnp.float32)
    for column in range(hard_ids.shape[1]):
        hardness_tally = hardness_tally + (hard_ids[:, column][:, None] == columns[None, :]).astype(jnp.float32)
    request_raw_similarity = request_similarity / sharpness_divisor + jnp.log1p(hardness_multiplier * hardness_tally)
    matching_indicator = positive[:, None] == columns[None, :]
    passage_raw_similarity = jnp.where(matching_indicator, -jnp.inf, passage_similarity / sharpness_divisor)
    row_peak = jnp.maximum(jnp.max(request_raw_similarity, axis=1), jnp.max(passage_raw_similarity, axis=1))
    row_mass = jnp.sum(jnp.exp(request_raw_similarity - row_peak[:, None]), axis=1) + jnp.sum(jnp.exp(passage_raw_similarity - row_peak[:, None]), axis=1)
    row_lse = row_peak + jnp.log(row_mass)
    loss_rows = row_lse - jnp.sum(jnp.where(matching_indicator, request_raw_similarity, 0.0), axis=1)
    request_probability = jnp.exp(request_raw_similarity - row_lse[:, None]).astype(jnp.bfloat16)
    passage_probability = jnp.exp(passage_raw_similarity - row_lse[:, None]).astype(jnp.bfloat16)
    return request_probability, passage_probability, loss_rows


def reference(queries, documents, positive, hard_ids):
    batch_size = documents.shape[0]
    request_matrix = queries.astype(jnp.bfloat16)
    passage_matrix = documents.astype(jnp.bfloat16)
    reference_side_entries = jnp.take(passage_matrix, positive, axis=0)
    request_similarity = jnp.dot(request_matrix, passage_matrix.T, preferred_element_type=jnp.float32)
    passage_similarity = jnp.dot(reference_side_entries, passage_matrix.T, preferred_element_type=jnp.float32)
    request_probability, passage_probability, loss_rows = weigh(request_similarity, passage_similarity, positive, hard_ids, batch_size)
    request_derivative = (jnp.dot(request_probability, passage_matrix, preferred_element_type=jnp.float32) - reference_side_entries.astype(jnp.float32)) / sharpness_divisor
    reference_side_derivative = jnp.dot(passage_probability, passage_matrix, preferred_element_type=jnp.float32) / sharpness_divisor
    forwarded_entries = reference_side_derivative - request_matrix.astype(jnp.float32) / sharpness_divisor
    dispersion_level = jnp.zeros(documents.shape, jnp.float32).at[positive].add(forwarded_entries)
    aggregate_loss = jnp.dot(request_probability.T, request_matrix, preferred_element_type=jnp.float32) + jnp.dot(passage_probability.T, reference_side_entries, preferred_element_type=jnp.float32)
    passage_derivative = aggregate_loss / sharpness_divisor + dispersion_level
    return request_derivative, passage_derivative, loss_rows
```

```python
import functools

import jax
import jax.numpy as jnp
from jax import lax
from jax.experimental import pallas as pl
from jax.experimental.pallas import tpu as pltpu
from jax.sharding import PartitionSpec as P

inverse_temperature = 20.0
hardness_multiplier = 3.0
MESH = pl.DeviceIdType.MESH
LANES = 128


def repeat(count, body):
    if count <= 8:
        for step in range(count):
            body(step)
    else:
        lax.fori_loop(0, count, lambda step, carry: (body(step), carry)[1], 0)


def kernel(
    n,
    q_hbm,
    d_hbm,
    pos_hbm,
    hid_hbm,
    req_ref,
    pas_ref,
    loss_ref,
    q_in,
    d_in,
    pos_in,
    hid_in,
    table,
    scores,
    landed,
    flipped,
    in_sem,
    send_sem,
    recv_sem,
    col_sem,
):
    rows, width = q_in.shape
    pair_rows = 2 * rows
    total = pair_rows * n
    chunks = total // LANES
    per_chunk = LANES // pair_rows
    me = lax.axis_index("row")
    core = lax.axis_index("col")
    depth = n // 2
    z, x = me // 2, me % 2
    twin = z * 2 + (1 - x)

    def line_peer(step):
        return lax.rem(z + step + 1, depth) * 2 + x

    def line_source(step):
        return lax.rem(z + depth - step - 1, depth) * 2 + x

    loads = [
        pltpu.make_async_copy(src, dst, in_sem.at[i])
        for i, (src, dst) in enumerate(
            ((pos_hbm, pos_in), (q_hbm, q_in), (d_hbm, d_in), (hid_hbm, hid_in))
        )
    ]
    for load in loads:
        load.start()

    barrier = pltpu.get_barrier_semaphore()

    def greet(step):
        pl.semaphore_signal(
            barrier, inc=1, device_id={"row": line_peer(step)}, device_id_type=MESH
        )

    repeat(depth - 1, greet)
    pl.semaphore_signal(barrier, inc=1, device_id={"row": twin}, device_id_type=MESH)
    pl.semaphore_signal(barrier, inc=1, device_id={"col": 1 - core}, device_id_type=MESH)

    for load in loads:
        load.wait()

    places = [pos_in[i] - me * rows for i in range(rows)]

    def to_documents(value):
        at = lax.broadcasted_iota(jnp.int32, value.shape, 0)
        out = jnp.zeros_like(value)
        for i in range(rows):
            out = jnp.where(at == places[i], value[i : i + 1, :], out)
        return out

    def to_queries(value):
        at = lax.broadcasted_iota(jnp.int32, value.shape, 0)
        place = jnp.zeros(value.shape, jnp.int32)
        for i in range(rows):
            place = jnp.where(at == i, places[i], place)
        out = jnp.zeros_like(value)
        for t in range(rows):
            out = jnp.where(place == t, value[t : t + 1, :], out)
        return out

    mine = pl.ds(pl.multiple_of(me * pair_rows, pair_rows), pair_rows)
    queries = to_documents(q_in[...])
    documents = d_in[...]
    lane = lax.broadcasted_iota(jnp.int32, (rows, total), 1)
    within = lax.rem(lane, pair_rows)
    document_id = jnp.where(
        within >= rows, lane // pair_rows * rows + within - rows, -1
    )
    hard = hid_in[...]
    tally = jnp.zeros((rows, total), jnp.float32)
    for k in range(hard.shape[1]):
        tally = tally + jnp.where(hard[:, k : k + 1] == document_id, 1.0, 0.0)
    table[mine, :width] = jnp.concatenate([queries, documents], axis=0).astype(jnp.bfloat16)
    table[mine, width:] = jnp.concatenate(
        [to_documents(tally), jnp.zeros_like(tally)], axis=0
    ).astype(jnp.bfloat16)

    pl.semaphore_wait(barrier, depth + 1)

    def block_copy(source, target, slot):
        block = table.at[pl.ds(pl.multiple_of(source * pair_rows, pair_rows), pair_rows)]
        return pltpu.make_async_remote_copy(
            src_ref=block,
            dst_ref=block,
            send_sem=send_sem.at[slot],
            recv_sem=recv_sem.at[source],
            device_id={"row": target},
            device_id_type=MESH,
        )

    block_copy(me, twin, 0).start()
    repeat(depth - 1, lambda step: block_copy(me, line_peer(step), 1 + step).start())

    def forward(step):
        source = line_source(step)
        block_copy(source, twin, depth + step).wait_recv()
        block_copy(source, twin, depth + step).start()

    repeat(depth - 1, forward)
    block_copy(twin, twin, 0).wait_recv()
    repeat(
        depth - 1,
        lambda step: block_copy(line_source(step) + 1 - 2 * x, twin, 0).wait_recv(),
    )

    def part(c):
        start = c * LANES
        return pl.ds(start if isinstance(c, int) else pl.multiple_of(start, LANES), LANES)

    def multiply(c):
        def against(e):
            scores[part(c), part(e)] = lax.dot_general(
                table[part(c), :width],
                table[part(e), :width],
                (((1,), (1,)), ((), ())),
                preferred_element_type=jnp.float32,
            )

        repeat(chunks, against)

    repeat(chunks, multiply)

    exchange = pltpu.make_async_remote_copy(
        src_ref=scores,
        dst_ref=landed,
        send_sem=col_sem.at[0],
        recv_sem=col_sem.at[1],
        device_id={"col": 1 - core},
        device_id_type=MESH,
    )
    exchange.start()

    half = (per_chunk, rows, total)
    column = lax.broadcasted_iota(jnp.int32, half, 2)
    is_document = lax.rem(column, pair_rows) >= rows
    own_column = (
        lax.broadcasted_iota(jnp.int32, half, 0) * pair_rows
        + lax.broadcasted_iota(jnp.int32, half, 1)
        + rows
    )

    def bias_of(c):
        counts = table[part(c), width:].astype(jnp.float32)
        counts = counts.reshape(per_chunk, pair_rows, total)[:, :rows]
        return jnp.log(1.0 + hardness_multiplier * counts)

    early = bias_of(0) if chunks == 1 else None
    exchange.wait()

    def weigh(c):
        bias = early if chunks == 1 else bias_of(c)
        logits = (scores[part(c), :] + landed[part(c), :]) * inverse_temperature
        logits = logits.reshape(per_chunk, pair_rows, total)
        is_positive = column == own_column + c * LANES
        query_logits = jnp.where(is_document, logits[:, :rows] + bias, -jnp.inf)
        doc_logits = jnp.where(
            is_document & jnp.logical_not(is_positive), logits[:, rows:], -jnp.inf
        )
        peak = jnp.max(jnp.maximum(query_logits, doc_logits), axis=2, keepdims=True)
        mass = jnp.sum(
            jnp.exp(query_logits - peak) + jnp.exp(doc_logits - peak), axis=2, keepdims=True
        )
        lse = peak + jnp.log(mass)
        losses = lse - jnp.sum(jnp.where(is_positive, query_logits, 0.0), axis=2, keepdims=True)
        weights = jnp.concatenate(
            [jnp.exp(query_logits - lse), jnp.exp(doc_logits - lse)], axis=1
        )
        scores[part(c), :] = weights.reshape(LANES, total)
        landed[part(c), :LANES] = jnp.broadcast_to(
            jnp.concatenate([losses, losses], axis=1), (per_chunk, pair_rows, LANES)
        ).reshape(LANES, LANES)

    repeat(chunks, weigh)

    upper = pl.ds(pl.multiple_of(me * pair_rows, rows), rows)
    lower = pl.ds(pl.multiple_of(me * pair_rows + rows, rows), rows)
    query_part = to_queries(scores[upper, :])
    doc_part = scores[lower, :]
    own_tile = pl.ds(pl.multiple_of(me // per_chunk * LANES, LANES), LANES)
    own_rows = pl.ds(
        pl.multiple_of(lax.rem(me, per_chunk) * pair_rows + rows, rows), rows
    )

    losses = landed[upper, :LANES]
    at = lax.broadcasted_iota(jnp.int32, losses.shape, 0)
    across = lax.broadcasted_iota(jnp.int32, losses.shape, 1)
    place = jnp.full(losses.shape, -1, jnp.int32)
    for i in range(rows):
        place = jnp.where(across == i, places[i], place)
    loss_ref[...] = jnp.sum(jnp.where(place == at, losses, 0.0), axis=0, keepdims=True)[:, :rows]

    if chunks > 1:
        landed[: 2 * rows, :total] = jnp.concatenate([query_part, doc_part], axis=0)
        req_ref[...] = jnp.zeros_like(req_ref)
        pas_ref[...] = jnp.zeros_like(pas_ref)

    def derive(c):
        flipped[...] = scores[part(c), own_tile].T
        if chunks > 1:
            heads = landed[: 2 * rows, part(c)]
        else:
            heads = jnp.concatenate([query_part, doc_part], axis=0)
        left = jnp.concatenate([heads, flipped[own_rows, :]], axis=0)
        out = jnp.dot(
            left.astype(jnp.bfloat16), table[part(c), :width], preferred_element_type=jnp.float32
        )
        request, passage = out[:rows], out[rows : 2 * rows] + out[2 * rows :]
        if chunks > 1:
            request, passage = req_ref[...] + request, pas_ref[...] + passage
        if chunks == 1 or isinstance(c, int):
            pass
        req_ref[...] = request
        pas_ref[...] = passage

    repeat(chunks, derive)
    own = table[mine, :width].astype(jnp.float32)
    req_ref[...] = (req_ref[...] - to_queries(own[rows:])) * inverse_temperature
    pas_ref[...] = (pas_ref[...] - own[:rows]) * inverse_temperature

    block_copy(me, twin, 0).wait_send()
    repeat(depth - 1, lambda step: block_copy(me, twin, 1 + step).wait_send())
    repeat(depth - 1, lambda step: block_copy(me, twin, depth + step).wait_send())


def on_device(queries, documents, positive, hard_ids):
    n = lax.axis_size("row")
    rows, width = queries.shape
    total = 2 * rows * n
    vmem = pl.BlockSpec(memory_space=pltpu.VMEM)
    request, passage, losses = pl.pallas_call(
        functools.partial(kernel, n),
        out_shape=(
            jax.ShapeDtypeStruct((rows, width), jnp.float32),
            jax.ShapeDtypeStruct((rows, width), jnp.float32),
            jax.ShapeDtypeStruct((1, rows), jnp.float32),
        ),
        in_specs=[pl.BlockSpec(memory_space=pl.ANY)] * 4,
        out_specs=(vmem, vmem, vmem),
        scratch_shapes=[
            pltpu.VMEM((rows, width), jnp.float32),
            pltpu.VMEM((rows, width), jnp.float32),
            pltpu.SMEM((rows,), jnp.int32),
            pltpu.VMEM(hard_ids.shape, jnp.int32),
            pltpu.VMEM((total, width + total), jnp.bfloat16),
            pltpu.VMEM((total, total), jnp.float32),
            pltpu.VMEM((total, total), jnp.float32),
            pltpu.VMEM((LANES, LANES), jnp.float32),
            pltpu.SemaphoreType.DMA((4,)),
            pltpu.SemaphoreType.DMA((n - 1,)),
            pltpu.SemaphoreType.DMA((n,)),
            pltpu.SemaphoreType.DMA((2,)),
        ],
        compiler_params=pltpu.CompilerParams(
            collective_id=0, has_side_effects=True, vmem_limit_bytes=60 * 1024 * 1024
        ),
    )(queries, documents, positive, hard_ids)
    return request, passage, losses.reshape(rows)


def solution(mesh):
    return jax.shard_map(
        on_device,
        mesh=mesh,
        in_specs=(
            P(("groups", "row"), "col"),
            P(("groups", "row"), "col"),
            P(("groups", "row")),
            P(("groups", "row"), None),
        ),
        out_specs=(P(("groups", "row"), "col"), P(("groups", "row"), "col"), P(("groups", "row"))),
        check_vma=False,
    )
```

```python
import functools

import jax
import jax.numpy as jnp
from jax import lax
from jax.experimental import pallas as pl
from jax.experimental.pallas import tpu as pltpu
from jax.sharding import PartitionSpec as P

inverse_temperature = 20.0
hardness_multiplier = 3.0
MESH = pl.DeviceIdType.MESH
LANES = 128
PIECES = 2


def repeat(count, body):
    if count <= 8:
        for step in range(count):
            body(step)
    else:
        lax.fori_loop(0, count, lambda step, carry: (body(step), carry)[1], 0)


def kernel(
    n,
    q_hbm,
    d_hbm,
    pos_hbm,
    hid_hbm,
    table,
    left_ref,
    loss_ref,
    q_in,
    d_in,
    pos_in,
    hid_in,
    scores,
    landed,
    flipped,
    in_sem,
    send_sem,
    recv_sem,
    col_sem,
):
    rows, width = q_in.shape
    pair_rows = 2 * rows
    total = pair_rows * n
    chunks = total // LANES
    per_chunk = LANES // pair_rows
    me = lax.axis_index("row")
    core = lax.axis_index("col")
    depth = n // 2
    z, x = me // 2, me % 2
    twin = z * 2 + (1 - x)

    def line_peer(step):
        return lax.rem(z + step + 1, depth) * 2 + x

    def line_source(step):
        return lax.rem(z + depth - step - 1, depth) * 2 + x

    loads = [
        pltpu.make_async_copy(src, dst, in_sem.at[i])
        for i, (src, dst) in enumerate(
            ((pos_hbm, pos_in), (q_hbm, q_in), (d_hbm, d_in), (hid_hbm, hid_in))
        )
    ]
    for load in loads:
        load.start()

    barrier = pltpu.get_barrier_semaphore()

    def greet(step):
        pl.semaphore_signal(
            barrier, inc=1, device_id={"row": line_peer(step)}, device_id_type=MESH
        )

    repeat(depth - 1, greet)
    pl.semaphore_signal(barrier, inc=1, device_id={"row": twin}, device_id_type=MESH)
    pl.semaphore_signal(barrier, inc=1, device_id={"col": 1 - core}, device_id_type=MESH)

    for load in loads:
        load.wait()

    places = [pos_in[i] - me * rows for i in range(rows)]

    def to_documents(value):
        at = lax.broadcasted_iota(jnp.int32, value.shape, 0)
        out = jnp.zeros_like(value)
        for i in range(rows):
            out = jnp.where(at == places[i], value[i : i + 1, :], out)
        return out

    def to_queries(value):
        at = lax.broadcasted_iota(jnp.int32, value.shape, 0)
        place = jnp.zeros(value.shape, jnp.int32)
        for i in range(rows):
            place = jnp.where(at == i, places[i], place)
        out = jnp.zeros_like(value)
        for t in range(rows):
            out = jnp.where(place == t, value[t : t + 1, :], out)
        return out

    mine = pl.ds(pl.multiple_of(me * pair_rows, pair_rows), pair_rows)
    queries = to_documents(q_in[...])
    documents = d_in[...]
    lane = lax.broadcasted_iota(jnp.int32, (rows, total), 1)
    within = lane & (pair_rows - 1)
    document_id = jnp.where(
        within >= rows, (lane - within) // 2 + within - rows, -1
    )
    hard = hid_in[...]
    tally = jnp.zeros((rows, total), jnp.float32)
    for k in range(hard.shape[1]):
        tally = tally + jnp.where(hard[:, k : k + 1] == document_id, 1.0, 0.0)
    table[mine, :width] = jnp.concatenate([queries, documents], axis=0).astype(jnp.bfloat16)
    table[mine, width:] = jnp.concatenate(
        [to_documents(tally), jnp.zeros_like(tally)], axis=0
    ).astype(jnp.bfloat16)

    pl.semaphore_wait(barrier, depth + 1)

    def block_copy(source, target, slot):
        block = table.at[pl.ds(pl.multiple_of(source * pair_rows, pair_rows), pair_rows)]
        return pltpu.make_async_remote_copy(
            src_ref=block,
            dst_ref=block,
            send_sem=send_sem.at[slot],
            recv_sem=recv_sem.at[source],
            device_id={"row": target},
            device_id_type=MESH,
        )

    block_copy(me, twin, 0).start()
    repeat(depth - 1, lambda step: block_copy(me, line_peer(step), 1 + step).start())

    def forward(step):
        source = line_source(step)
        block_copy(source, twin, depth + step).wait_recv()
        block_copy(source, twin, depth + step).start()

    repeat(depth - 1, forward)
    block_copy(twin, twin, 0).wait_recv()
    repeat(
        depth - 1,
        lambda step: block_copy(line_source(step) + 1 - 2 * x, twin, 0).wait_recv(),
    )

    def part(c):
        start = c * LANES
        return pl.ds(start if isinstance(c, int) else pl.multiple_of(start, LANES), LANES)

    def multiply(c):
        def against(e):
            scores[part(c), part(e)] = lax.dot_general(
                table[part(c), :width],
                table[part(e), :width],
                (((1,), (1,)), ((), ())),
                preferred_element_type=jnp.float32,
            )

        repeat(chunks, against)

    repeat(chunks, multiply)

    exchange = pltpu.make_async_remote_copy(
        src_ref=scores,
        dst_ref=landed,
        send_sem=col_sem.at[0],
        recv_sem=col_sem.at[1],
        device_id={"col": 1 - core},
        device_id_type=MESH,
    )
    exchange.start()

    half = (per_chunk, rows, total)
    column = lax.broadcasted_iota(jnp.int32, half, 2)
    is_document = (column & rows) != 0
    own_column = (
        lax.broadcasted_iota(jnp.int32, half, 0) * pair_rows
        + lax.broadcasted_iota(jnp.int32, half, 1)
        + rows
    )

    def bias_of(c):
        counts = table[part(c), width:].astype(jnp.float32)
        counts = counts.reshape(per_chunk, pair_rows, total)[:, :rows]
        return jnp.log(1.0 + hardness_multiplier * counts)

    tile = (rows, LANES)
    tile_row = lax.broadcasted_iota(jnp.int32, tile, 0)
    tile_lane = lax.broadcasted_iota(jnp.int32, tile, 1)
    across_place = jnp.full(tile, -1, jnp.int32)
    down_place = jnp.zeros(tile, jnp.int32)
    for i in range(rows):
        across_place = jnp.where(tile_lane == i, places[i], across_place)
        down_place = jnp.where(tile_row == i, places[i], down_place)

    def anchor_rows(c):
        at = tile_lane + c * LANES - (me * pair_rows + rows)
        return jnp.where(at == down_place, -1.0, 0.0)

    early = bias_of(0) if chunks == 1 else None
    exchange.wait()

    def weigh(c):
        bias = early if chunks == 1 else bias_of(c)
        logits = (scores[part(c), :] + landed[part(c), :]) * inverse_temperature
        logits = logits.reshape(per_chunk, pair_rows, total)
        is_positive = column == own_column + c * LANES
        query_logits = jnp.where(is_document, logits[:, :rows] + bias, -jnp.inf)
        doc_logits = jnp.where(
            is_document & jnp.logical_not(is_positive), logits[:, rows:], -jnp.inf
        )
        peak = jnp.max(jnp.maximum(query_logits, doc_logits), axis=2, keepdims=True)
        mass = jnp.sum(
            jnp.exp(query_logits - peak) + jnp.exp(doc_logits - peak), axis=2, keepdims=True
        )
        lse = peak + jnp.log(mass)
        losses = lse - jnp.sum(jnp.where(is_positive, query_logits, 0.0), axis=2, keepdims=True)
        weights = jnp.concatenate(
            [jnp.exp(query_logits - lse), jnp.exp(doc_logits - lse)], axis=1
        )
        scores[part(c), :] = weights.reshape(LANES, total)
        landed[part(c), :LANES] = jnp.broadcast_to(
            jnp.concatenate([losses, losses], axis=1), (per_chunk, pair_rows, LANES)
        ).reshape(LANES, LANES)

    repeat(chunks, weigh)

    upper = pl.ds(pl.multiple_of(me * pair_rows, rows), rows)
    lower = pl.ds(pl.multiple_of(me * pair_rows + rows, rows), rows)
    sublane = lax.broadcasted_iota(jnp.int32, (rows, total), 0)
    heads = jnp.where(lane == me * pair_rows + sublane, -1.0, scores[lower, :])
    left_ref[: 2 * rows, :] = jnp.concatenate(
        [to_queries(scores[upper, :]), heads], axis=0
    ).astype(jnp.bfloat16)
    own_tile = pl.ds(pl.multiple_of(me // per_chunk * LANES, LANES), LANES)
    own_rows = pl.ds(
        pl.multiple_of(lax.rem(me, per_chunk) * pair_rows + rows, rows), rows
    )

    def columns(c):
        flipped[...] = scores[part(c), own_tile].T
        left_ref[2 * rows :, part(c)] = jnp.concatenate(
            [flipped[own_rows, :], anchor_rows(c)], axis=0
        ).astype(jnp.bfloat16)

    repeat(chunks, columns)

    losses = landed[upper, :LANES]
    at = lax.broadcasted_iota(jnp.int32, losses.shape, 0)
    loss_ref[...] = jnp.sum(jnp.where(across_place == at, losses, 0.0), axis=0, keepdims=True)

    block_copy(me, twin, 0).wait_send()
    repeat(depth - 1, lambda step: block_copy(me, twin, 1 + step).wait_send())
    repeat(depth - 1, lambda step: block_copy(me, twin, depth + step).wait_send())


def finish(width, left_ref, table_ref, loss_in, req_hbm, pas_hbm, loss_ref, req, pas, sem):
    rows = req.shape[0]
    loss_ref[...] = loss_in[0, :rows]
    total = left_ref.shape[1]
    step = width // PIECES
    copies = []
    for piece in range(PIECES):
        across = pl.ds(piece * step, step)
        out = jnp.zeros((4 * rows, step), jnp.float32)
        for start in range(0, total, LANES):
            depth = min(total, LANES)
            out = out + jnp.dot(
                left_ref[:, start : start + depth],
                table_ref[start : start + depth, across],
                preferred_element_type=jnp.float32,
            )
        req[:, across] = (out[:rows] + out[3 * rows :]) * inverse_temperature
        pas[:, across] = (out[rows : 2 * rows] + out[2 * rows : 3 * rows]) * inverse_temperature
        for which, (src, dst) in enumerate(((req, req_hbm), (pas, pas_hbm))):
            copy = pltpu.make_async_copy(
                src.at[:, across], dst.at[:, across], sem.at[2 * piece + which]
            )
            copy.start()
            copies.append(copy)
    for copy in copies:
        copy.wait()


def on_device(queries, documents, positive, hard_ids):
    n = lax.axis_size("row")
    rows, width = queries.shape
    total = 2 * rows * n
    vmem = pl.BlockSpec(memory_space=pltpu.VMEM)
    anywhere = pl.BlockSpec(memory_space=pl.ANY)
    inputs = (queries, documents, positive, hard_ids)
    table, left, losses = pl.pallas_call(
        functools.partial(kernel, n),
        out_shape=(
            pltpu.VMEM((total, width + total), jnp.bfloat16),
            pltpu.VMEM((4 * rows, total), jnp.bfloat16),
            pltpu.VMEM((1, LANES), jnp.float32),
        ),
        in_specs=[anywhere] * 4,
        out_specs=(vmem, vmem, vmem),
        scratch_shapes=[
            pltpu.VMEM((rows, width), jnp.float32),
            pltpu.VMEM((rows, width), jnp.float32),
            pltpu.SMEM((rows,), jnp.int32),
            pltpu.VMEM(hard_ids.shape, jnp.int32),
            pltpu.VMEM((total, total), jnp.float32),
            pltpu.VMEM((total, total), jnp.float32),
            pltpu.VMEM((LANES, LANES), jnp.float32),
            pltpu.SemaphoreType.DMA((4,)),
            pltpu.SemaphoreType.DMA((n - 1,)),
            pltpu.SemaphoreType.DMA((n,)),
            pltpu.SemaphoreType.DMA((2,)),
        ],
        compiler_params=pltpu.CompilerParams(
            collective_id=0,
            has_side_effects=True,
            vmem_limit_bytes=8 * total * total + 6 * 1024 * 1024,
        ),
    )(*(pltpu.with_memory_space_constraint(a, pltpu.HBM) for a in inputs))
    table, left, losses = (
        pltpu.with_memory_space_constraint(a, pltpu.VMEM) for a in (table, left, losses)
    )
    return pl.pallas_call(
        functools.partial(finish, width),
        out_shape=(
            jax.ShapeDtypeStruct((rows, width), jnp.float32),
            jax.ShapeDtypeStruct((rows, width), jnp.float32),
            jax.ShapeDtypeStruct((rows,), jnp.float32),
        ),
        in_specs=[vmem] * 3,
        out_specs=(anywhere, anywhere, vmem),
        scratch_shapes=[
            pltpu.VMEM((rows, width), jnp.float32),
            pltpu.VMEM((rows, width), jnp.float32),
            pltpu.SemaphoreType.DMA((2 * PIECES,)),
        ],
        compiler_params=pltpu.CompilerParams(vmem_limit_bytes=6 * 1024 * 1024),
    )(left, table, losses)


def solution(mesh):
    return jax.shard_map(
        on_device,
        mesh=mesh,
        in_specs=(
            P(("groups", "row"), "col"),
            P(("groups", "row"), "col"),
            P(("groups", "row")),
            P(("groups", "row"), None),
        ),
        out_specs=(P(("groups", "row"), "col"), P(("groups", "row"), "col"), P(("groups", "row"))),
        check_vma=False,
    )
```

```python
import functools

import jax
import jax.numpy as jnp
from jax import lax
from jax.experimental import pallas as pl
from jax.experimental.pallas import tpu as pltpu
from jax.sharding import PartitionSpec as P

inverse_temperature = 20.0
hardness_multiplier = 3.0
MESH = pl.DeviceIdType.MESH
LANES = 128
PIECES = 2


def repeat(count, body):
    if count <= 8:
        for step in range(count):
            body(step)
    else:
        lax.fori_loop(0, count, lambda step, carry: (body(step), carry)[1], 0)


def kernel(
    n,
    q_hbm,
    d_hbm,
    pos_hbm,
    hid_hbm,
    table,
    left_ref,
    loss_ref,
    q_in,
    d_in,
    pos_in,
    hid_in,
    scores,
    landed,
    flipped,
    in_sem,
    up_sem,
    down_sem,
    side_sem,
    recv_sem,
    col_sem,
):
    rows, width = q_in.shape
    pair_rows = 2 * rows
    total = pair_rows * n
    chunks = total // LANES
    per_chunk = LANES // pair_rows
    me = lax.axis_index("row")
    core = lax.axis_index("col")
    depth = n // 2
    z, x = me // 2, me % 2
    twin = z * 2 + (1 - x)
    above, below = z + 1 < depth, z > 0

    def line(place):
        return place * 2 + x

    loads = [
        pltpu.make_async_copy(src, dst, in_sem.at[i])
        for i, (src, dst) in enumerate(
            ((pos_hbm, pos_in), (q_hbm, q_in), (d_hbm, d_in), (hid_hbm, hid_in))
        )
    ]
    for load in loads:
        load.start()

    barrier = pltpu.get_barrier_semaphore()

    def greet(device):
        pl.semaphore_signal(barrier, inc=1, device_id=device, device_id_type=MESH)

    greet({"row": twin})
    greet({"col": 1 - core})
    pl.when(above)(lambda: greet({"row": line(z + 1)}))
    pl.when(below)(lambda: greet({"row": line(z - 1)}))

    for load in loads:
        load.wait()

    places = [pos_in[i] - me * rows for i in range(rows)]

    def to_documents(value):
        at = lax.broadcasted_iota(jnp.int32, value.shape, 0)
        out = jnp.zeros_like(value)
        for i in range(rows):
            out = jnp.where(at == places[i], value[i : i + 1, :], out)
        return out

    def to_queries(value):
        at = lax.broadcasted_iota(jnp.int32, value.shape, 0)
        place = jnp.zeros(value.shape, jnp.int32)
        for i in range(rows):
            place = jnp.where(at == i, places[i], place)
        out = jnp.zeros_like(value)
        for t in range(rows):
            out = jnp.where(place == t, value[t : t + 1, :], out)
        return out

    mine = pl.ds(pl.multiple_of(me * pair_rows, pair_rows), pair_rows)
    queries = to_documents(q_in[...])
    documents = d_in[...]
    lane = lax.broadcasted_iota(jnp.int32, (rows, total), 1)
    within = lane & (pair_rows - 1)
    document_id = jnp.where(
        within >= rows, (lane - within) // 2 + within - rows, -1
    )
    hard = hid_in[...]
    tally = jnp.zeros((rows, total), jnp.float32)
    for k in range(hard.shape[1]):
        tally = tally + jnp.where(hard[:, k : k + 1] == document_id, 1.0, 0.0)
    table[mine, :width] = jnp.concatenate([queries, documents], axis=0).astype(jnp.bfloat16)
    table[mine, width:] = jnp.concatenate(
        [to_documents(tally), jnp.zeros_like(tally)], axis=0
    ).astype(jnp.bfloat16)

    pl.semaphore_wait(barrier, 2 + above.astype(jnp.int32) + below.astype(jnp.int32))

    halves = (pl.ds(0, width // 2), pl.ds(width // 2, width // 2 + total))

    def block_copy(source, half, target, sem):
        block = table.at[
            pl.ds(pl.multiple_of(source * pair_rows, pair_rows), pair_rows), halves[half]
        ]
        return pltpu.make_async_remote_copy(
            src_ref=block,
            dst_ref=block,
            send_sem=sem,
            recv_sem=recv_sem.at[source, half],
            device_id={"row": target},
            device_id_type=MESH,
        )

    def upward(place, half):
        return block_copy(line(place), half, line(z + 1), up_sem.at[place, half])

    def downward(place, half):
        return block_copy(line(place), half, line(z - 1), down_sem.at[place, half])

    def sideward(place, half):
        return block_copy(line(place), half, twin, side_sem.at[place, half])

    def arrival(source, half):
        block_copy(source, half, twin, side_sem.at[0, half]).wait_recv()

    for half in range(2):
        pl.when(above)(lambda: upward(z, half).start())
        pl.when(below)(lambda: downward(z, half).start())
        sideward(z, half).start()

    def relay(step):
        low, high = z - step - 1, z + step + 1
        for half in range(2):

            @pl.when(low >= 0)
            def _():
                arrival(line(low), half)
                pl.when(above)(lambda: upward(low, half).start())
                sideward(low, half).start()

            @pl.when(high < depth)
            def _():
                arrival(line(high), half)
                pl.when(below)(lambda: downward(high, half).start())
                sideward(high, half).start()

    repeat(depth - 1, relay)

    def part(c):
        start = c * LANES
        return pl.ds(start if isinstance(c, int) else pl.multiple_of(start, LANES), LANES)

    for half in range(2):
        repeat(depth, lambda place: arrival(place * 2 + 1 - x, half))
        features = slice(half * width // 2, (half + 1) * width // 2)

        def multiply(c):
            def against(e):
                product = lax.dot_general(
                    table[part(c), features],
                    table[part(e), features],
                    (((1,), (1,)), ((), ())),
                    preferred_element_type=jnp.float32,
                )
                if half == 1:
                    product = product + scores[part(c), part(e)]
                scores[part(c), part(e)] = product

            repeat(chunks, against)

        repeat(chunks, multiply)

    exchange = pltpu.make_async_remote_copy(
        src_ref=scores,
        dst_ref=landed,
        send_sem=col_sem.at[0],
        recv_sem=col_sem.at[1],
        device_id={"col": 1 - core},
        device_id_type=MESH,
    )
    exchange.start()

    half = (per_chunk, rows, total)
    column = lax.broadcasted_iota(jnp.int32, half, 2)
    is_document = (column & rows) != 0
    own_column = (
        lax.broadcasted_iota(jnp.int32, half, 0) * pair_rows
        + lax.broadcasted_iota(jnp.int32, half, 1)
        + rows
    )

    def bias_of(c):
        counts = table[part(c), width:].astype(jnp.float32)
        counts = counts.reshape(per_chunk, pair_rows, total)[:, :rows]
        return jnp.log(1.0 + hardness_multiplier * counts)

    tile = (rows, LANES)
    tile_row = lax.broadcasted_iota(jnp.int32, tile, 0)
    tile_lane = lax.broadcasted_iota(jnp.int32, tile, 1)
    across_place = jnp.full(tile, -1, jnp.int32)
    down_place = jnp.zeros(tile, jnp.int32)
    for i in range(rows):
        across_place = jnp.where(tile_lane == i, places[i], across_place)
        down_place = jnp.where(tile_row == i, places[i], down_place)

    def anchor_rows(c):
        at = tile_lane + c * LANES - (me * pair_rows + rows)
        return jnp.where(at == down_place, -1.0, 0.0)

    early = bias_of(0) if chunks == 1 else None
    exchange.wait()

    def weigh(c):
        bias = early if chunks == 1 else bias_of(c)
        logits = (scores[part(c), :] + landed[part(c), :]) * inverse_temperature
        logits = logits.reshape(per_chunk, pair_rows, total)
        is_positive = column == own_column + c * LANES
        query_logits = jnp.where(is_document, logits[:, :rows] + bias, -jnp.inf)
        doc_logits = jnp.where(
            is_document & jnp.logical_not(is_positive), logits[:, rows:], -jnp.inf
        )
        peak = jnp.max(jnp.maximum(query_logits, doc_logits), axis=2, keepdims=True)
        query_terms, doc_terms = jnp.exp(query_logits - peak), jnp.exp(doc_logits - peak)
        mass = jnp.sum(query_terms + doc_terms, axis=2, keepdims=True)
        lse = peak + jnp.log(mass)
        share = 1.0 / mass
        losses = lse - jnp.sum(jnp.where(is_positive, query_logits, 0.0), axis=2, keepdims=True)
        weights = jnp.concatenate(
            [query_terms * share, doc_terms * share], axis=1
        )
        scores[part(c), :] = weights.reshape(LANES, total)
        landed[part(c), :LANES] = jnp.broadcast_to(
            jnp.concatenate([losses, losses], axis=1), (per_chunk, pair_rows, LANES)
        ).reshape(LANES, LANES)

    repeat(chunks, weigh)

    upper = pl.ds(pl.multiple_of(me * pair_rows, rows), rows)
    lower = pl.ds(pl.multiple_of(me * pair_rows + rows, rows), rows)
    sublane = lax.broadcasted_iota(jnp.int32, (rows, total), 0)
    heads = jnp.where(lane == me * pair_rows + sublane, -1.0, scores[lower, :])
    left_ref[: 2 * rows, :] = jnp.concatenate(
        [to_queries(scores[upper, :]), heads], axis=0
    ).astype(jnp.bfloat16)
    own_tile = pl.ds(pl.multiple_of(me // per_chunk * LANES, LANES), LANES)
    own_rows = pl.ds(
        pl.multiple_of(lax.rem(me, per_chunk) * pair_rows + rows, rows), rows
    )

    def columns(c):
        flipped[...] = scores[part(c), own_tile].T
        left_ref[2 * rows :, part(c)] = jnp.concatenate(
            [flipped[own_rows, :], anchor_rows(c)], axis=0
        ).astype(jnp.bfloat16)

    repeat(chunks, columns)

    losses = landed[upper, :LANES]
    at = lax.broadcasted_iota(jnp.int32, losses.shape, 0)
    loss_ref[...] = jnp.sum(jnp.where(across_place == at, losses, 0.0), axis=0, keepdims=True)

    def drain(place):
        for half in range(2):
            sideward(place, half).wait_send()
            pl.when(above & (place <= z))(lambda: upward(place, half).wait_send())
            pl.when(below & (place >= z))(lambda: downward(place, half).wait_send())

    repeat(depth, drain)


def finish(width, left_ref, table_ref, loss_in, req_hbm, pas_hbm, loss_hbm, req, pas, loss, sem):
    rows = req.shape[0]
    loss[...] = loss_in[:, :rows]
    loss_copy = pltpu.make_async_copy(loss, loss_hbm, sem.at[2 * PIECES])
    loss_copy.start()
    total = left_ref.shape[1]
    step = width // PIECES
    copies = [loss_copy]
    for piece in range(PIECES):
        across = pl.ds(piece * step, step)
        out = jnp.zeros((4 * rows, step), jnp.float32)
        for start in range(0, total, LANES):
            depth = min(total, LANES)
            out = out + jnp.dot(
                left_ref[:, start : start + depth],
                table_ref[start : start + depth, across],
                preferred_element_type=jnp.float32,
            )
        req[:, across] = (out[:rows] + out[3 * rows :]) * inverse_temperature
        pas[:, across] = (out[rows : 2 * rows] + out[2 * rows : 3 * rows]) * inverse_temperature
        for which, (src, dst) in enumerate(((req, req_hbm), (pas, pas_hbm))):
            copy = pltpu.make_async_copy(
                src.at[:, across], dst.at[:, across], sem.at[2 * piece + which]
            )
            copy.start()
            copies.append(copy)
    for copy in copies:
        copy.wait()


def on_device(queries, documents, positive, hard_ids):
    n = lax.axis_size("row")
    rows, width = queries.shape
    total = 2 * rows * n
    vmem = pl.BlockSpec(memory_space=pltpu.VMEM)
    anywhere = pl.BlockSpec(memory_space=pl.ANY)
    inputs = (queries, documents, positive, hard_ids)
    table, left, losses = pl.pallas_call(
        functools.partial(kernel, n),
        out_shape=(
            pltpu.VMEM((total, width + total), jnp.bfloat16),
            pltpu.VMEM((4 * rows, total), jnp.bfloat16),
            pltpu.VMEM((1, LANES), jnp.float32),
        ),
        in_specs=[anywhere] * 4,
        out_specs=(vmem, vmem, vmem),
        scratch_shapes=[
            pltpu.VMEM((rows, width), jnp.float32),
            pltpu.VMEM((rows, width), jnp.float32),
            pltpu.SMEM((rows,), jnp.int32),
            pltpu.VMEM(hard_ids.shape, jnp.int32),
            pltpu.VMEM((total, total), jnp.float32),
            pltpu.VMEM((total, total), jnp.float32),
            pltpu.VMEM((LANES, LANES), jnp.float32),
            pltpu.SemaphoreType.DMA((4,)),
            pltpu.SemaphoreType.DMA((n // 2, 2)),
            pltpu.SemaphoreType.DMA((n // 2, 2)),
            pltpu.SemaphoreType.DMA((n // 2, 2)),
            pltpu.SemaphoreType.DMA((n, 2)),
            pltpu.SemaphoreType.DMA((2,)),
        ],
        compiler_params=pltpu.CompilerParams(
            collective_id=0,
            has_side_effects=True,
            vmem_limit_bytes=8 * total * total + 6 * 1024 * 1024,
        ),
    )(*(pltpu.with_memory_space_constraint(a, pltpu.HBM) for a in inputs))
    table, left, losses = (
        pltpu.with_memory_space_constraint(a, pltpu.VMEM) for a in (table, left, losses)
    )
    request, passage, losses = pl.pallas_call(
        functools.partial(finish, width),
        out_shape=(
            jax.ShapeDtypeStruct((rows, width), jnp.float32),
            jax.ShapeDtypeStruct((rows, width), jnp.float32),
            jax.ShapeDtypeStruct((1, rows), jnp.float32),
        ),
        in_specs=[vmem] * 3,
        out_specs=(anywhere,) * 3,
        scratch_shapes=[
            pltpu.VMEM((rows, width), jnp.float32),
            pltpu.VMEM((rows, width), jnp.float32),
            pltpu.VMEM((1, rows), jnp.float32),
            pltpu.SemaphoreType.DMA((2 * PIECES + 1,)),
        ],
        compiler_params=pltpu.CompilerParams(vmem_limit_bytes=6 * 1024 * 1024),
    )(left, table, losses)
    return request, passage, losses.reshape(rows)


def solution(mesh):
    return jax.shard_map(
        on_device,
        mesh=mesh,
        in_specs=(
            P(("groups", "row"), "col"),
            P(("groups", "row"), "col"),
            P(("groups", "row")),
            P(("groups", "row"), None),
        ),
        out_specs=(P(("groups", "row"), "col"), P(("groups", "row"), "col"), P(("groups", "row"))),
        check_vma=False,
    )
```

```python
import functools

import jax
import jax.numpy as jnp
from jax import lax
from jax.experimental import pallas as pl
from jax.experimental.pallas import tpu as pltpu
from jax.sharding import PartitionSpec as P

inverse_temperature = 20.0
hardness_multiplier = 3.0
MESH = pl.DeviceIdType.MESH
LANES = 128
PIECES = 2


def repeat(count, body):
    if count <= 8:
        for step in range(count):
            body(step)
    else:
        lax.fori_loop(0, count, lambda step, carry: (body(step), carry)[1], 0)


def kernel(
    n,
    q_hbm,
    d_hbm,
    pos_hbm,
    hid_hbm,
    table,
    left_ref,
    loss_ref,
    q_in,
    d_in,
    pos_in,
    hid_in,
    scores,
    landed,
    flipped,
    in_sem,
    up_sem,
    down_sem,
    side_sem,
    recv_sem,
    col_sem,
):
    rows, width = q_in.shape
    pair_rows = 2 * rows
    total = pair_rows * n
    chunks = total // LANES
    per_chunk = LANES // pair_rows
    me = lax.axis_index("row")
    core = lax.axis_index("col")
    depth = n // 2
    z, x = me // 2, me % 2
    twin = z * 2 + (1 - x)

    def line(place):
        return place * 2 + x

    loads = [
        pltpu.make_async_copy(src, dst, in_sem.at[i])
        for i, (src, dst) in enumerate(
            ((pos_hbm, pos_in), (q_hbm, q_in), (d_hbm, d_in), (hid_hbm, hid_in))
        )
    ]
    for load in loads:
        load.start()

    barrier = pltpu.get_barrier_semaphore()

    def greet(device):
        pl.semaphore_signal(barrier, inc=1, device_id=device, device_id_type=MESH)

    greet({"row": twin})
    greet({"col": 1 - core})

    def greet_line(step):
        high, low = z + step + 1, z - step - 1
        pl.when(high < depth)(lambda: greet({"row": line(high)}))
        pl.when(low >= 0)(lambda: greet({"row": line(low)}))

    repeat(depth - 1, greet_line)

    for load in loads:
        load.wait()

    places = [pos_in[i] - me * rows for i in range(rows)]

    def to_documents(value):
        at = lax.broadcasted_iota(jnp.int32, value.shape, 0)
        out = jnp.zeros_like(value)
        for i in range(rows):
            out = jnp.where(at == places[i], value[i : i + 1, :], out)
        return out

    def to_queries(value):
        at = lax.broadcasted_iota(jnp.int32, value.shape, 0)
        place = jnp.zeros(value.shape, jnp.int32)
        for i in range(rows):
            place = jnp.where(at == i, places[i], place)
        out = jnp.zeros_like(value)
        for t in range(rows):
            out = jnp.where(place == t, value[t : t + 1, :], out)
        return out

    mine = pl.ds(pl.multiple_of(me * pair_rows, pair_rows), pair_rows)
    queries = to_documents(q_in[...])
    documents = d_in[...]
    lane = lax.broadcasted_iota(jnp.int32, (rows, total), 1)
    within = lane & (pair_rows - 1)
    document_id = jnp.where(
        within >= rows, (lane - within) // 2 + within - rows, -1
    )
    hard = hid_in[...]
    tally = jnp.zeros((rows, total), jnp.float32)
    for k in range(hard.shape[1]):
        tally = tally + jnp.where(hard[:, k : k + 1] == document_id, 1.0, 0.0)
    table[mine, :width] = jnp.concatenate([queries, documents], axis=0).astype(jnp.bfloat16)
    table[mine, width:] = jnp.concatenate(
        [to_documents(tally), jnp.zeros_like(tally)], axis=0
    ).astype(jnp.bfloat16)

    pl.semaphore_wait(barrier, depth + 1)

    halves = (pl.ds(0, width // 2), pl.ds(width // 2, width // 2 + total))

    def block_copy(source, half, target, sem):
        block = table.at[
            pl.ds(pl.multiple_of(source * pair_rows, pair_rows), pair_rows), halves[half]
        ]
        return pltpu.make_async_remote_copy(
            src_ref=block,
            dst_ref=block,
            send_sem=sem,
            recv_sem=recv_sem.at[source, half],
            device_id={"row": target},
            device_id_type=MESH,
        )

    def upward(far, half):
        return block_copy(me, half, line(z + far), up_sem.at[far, half])

    def downward(far, half):
        return block_copy(me, half, line(z - far), down_sem.at[far, half])

    def along(far, act):
        for half in range(2):
            pl.when(z + far < depth)(lambda: act(upward(far, half)))
            pl.when(z - far >= 0)(lambda: act(downward(far, half)))

    def sideward(place, half):
        return block_copy(line(place), half, twin, side_sem.at[place, half])

    def arrival(source, half):
        block_copy(source, half, twin, side_sem.at[0, half]).wait_recv()

    along(1, lambda copy: copy.start())
    for half in range(2):
        sideward(z, half).start()

    def relay(step):
        low, high = z - step - 1, z + step + 1
        for half in range(2):

            @pl.when(low >= 0)
            def _():
                arrival(line(low), half)
                sideward(low, half).start()

            @pl.when(high < depth)
            def _():
                arrival(line(high), half)
                sideward(high, half).start()

            if half == 0:
                along(step + 2, lambda copy: copy.start())

    repeat(depth - 1, relay)

    def part(c):
        start = c * LANES
        return pl.ds(start if isinstance(c, int) else pl.multiple_of(start, LANES), LANES)

    for half in range(2):
        repeat(depth, lambda place: arrival(place * 2 + 1 - x, half))
        features = slice(half * width // 2, (half + 1) * width // 2)

        def multiply(c):
            def against(e):
                product = lax.dot_general(
                    table[part(c), features],
                    table[part(e), features],
                    (((1,), (1,)), ((), ())),
                    preferred_element_type=jnp.float32,
                )
                if half == 1:
                    product = product + scores[part(c), part(e)]
                scores[part(c), part(e)] = product

            repeat(chunks, against)

        repeat(chunks, multiply)

    exchange = pltpu.make_async_remote_copy(
        src_ref=scores,
        dst_ref=landed,
        send_sem=col_sem.at[0],
        recv_sem=col_sem.at[1],
        device_id={"col": 1 - core},
        device_id_type=MESH,
    )
    exchange.start()

    half = (per_chunk, rows, total)
    column = lax.broadcasted_iota(jnp.int32, half, 2)
    is_document = (column & rows) != 0
    own_column = (
        lax.broadcasted_iota(jnp.int32, half, 0) * pair_rows
        + lax.broadcasted_iota(jnp.int32, half, 1)
        + rows
    )

    def bias_of(c):
        counts = table[part(c), width:].astype(jnp.float32)
        counts = counts.reshape(per_chunk, pair_rows, total)[:, :rows]
        return jnp.log(1.0 + hardness_multiplier * counts)

    tile = (rows, LANES)
    tile_row = lax.broadcasted_iota(jnp.int32, tile, 0)
    tile_lane = lax.broadcasted_iota(jnp.int32, tile, 1)
    across_place = jnp.full(tile, -1, jnp.int32)
    down_place = jnp.zeros(tile, jnp.int32)
    for i in range(rows):
        across_place = jnp.where(tile_lane == i, places[i], across_place)
        down_place = jnp.where(tile_row == i, places[i], down_place)

    def anchor_rows(c):
        at = tile_lane + c * LANES - (me * pair_rows + rows)
        return jnp.where(at == down_place, -1.0, 0.0)

    early = bias_of(0) if chunks == 1 else None
    exchange.wait()

    def weigh(c):
        bias = early if chunks == 1 else bias_of(c)
        logits = (scores[part(c), :] + landed[part(c), :]) * inverse_temperature
        logits = logits.reshape(per_chunk, pair_rows, total)
        is_positive = column == own_column + c * LANES
        query_logits = jnp.where(is_document, logits[:, :rows] + bias, -jnp.inf)
        doc_logits = jnp.where(
            is_document & jnp.logical_not(is_positive), logits[:, rows:], -jnp.inf
        )
        peak = jnp.max(jnp.maximum(query_logits, doc_logits), axis=2, keepdims=True)
        query_terms, doc_terms = jnp.exp(query_logits - peak), jnp.exp(doc_logits - peak)
        mass = jnp.sum(query_terms + doc_terms, axis=2, keepdims=True)
        lse = peak + jnp.log(mass)
        share = 1.0 / mass
        losses = lse - jnp.sum(jnp.where(is_positive, query_logits, 0.0), axis=2, keepdims=True)
        weights = jnp.concatenate(
            [query_terms * share, doc_terms * share], axis=1
        )
        scores[part(c), :] = weights.reshape(LANES, total)
        landed[part(c), :LANES] = jnp.broadcast_to(
            jnp.concatenate([losses, losses], axis=1), (per_chunk, pair_rows, LANES)
        ).reshape(LANES, LANES)

    repeat(chunks, weigh)

    upper = pl.ds(pl.multiple_of(me * pair_rows, rows), rows)
    lower = pl.ds(pl.multiple_of(me * pair_rows + rows, rows), rows)
    sublane = lax.broadcasted_iota(jnp.int32, (rows, total), 0)
    heads = jnp.where(lane == me * pair_rows + sublane, -1.0, scores[lower, :])
    left_ref[: 2 * rows, :] = jnp.concatenate(
        [to_queries(scores[upper, :]), heads], axis=0
    ).astype(jnp.bfloat16)
    own_tile = pl.ds(pl.multiple_of(me // per_chunk * LANES, LANES), LANES)
    own_rows = pl.ds(
        pl.multiple_of(lax.rem(me, per_chunk) * pair_rows + rows, rows), rows
    )

    def columns(c):
        flipped[...] = scores[part(c), own_tile].T
        left_ref[2 * rows :, part(c)] = jnp.concatenate(
            [flipped[own_rows, :], anchor_rows(c)], axis=0
        ).astype(jnp.bfloat16)

    repeat(chunks, columns)

    losses = landed[upper, :LANES]
    at = lax.broadcasted_iota(jnp.int32, losses.shape, 0)
    loss_ref[...] = jnp.sum(jnp.where(across_place == at, losses, 0.0), axis=0, keepdims=True)

    def drain(place):
        for half in range(2):
            sideward(place, half).wait_send()

    repeat(depth, drain)
    repeat(depth - 1, lambda step: along(step + 1, lambda copy: copy.wait_send()))


def finish(width, left_ref, table_ref, loss_in, req_hbm, pas_hbm, loss_hbm, req, pas, loss, sem):
    rows = req.shape[0]
    loss[...] = loss_in[:, :rows]
    loss_copy = pltpu.make_async_copy(loss, loss_hbm, sem.at[2 * PIECES])
    loss_copy.start()
    total = left_ref.shape[1]
    step = width // PIECES
    copies = [loss_copy]
    for piece in range(PIECES):
        across = pl.ds(piece * step, step)
        out = jnp.zeros((4 * rows, step), jnp.float32)
        for start in range(0, total, LANES):
            depth = min(total, LANES)
            out = out + jnp.dot(
                left_ref[:, start : start + depth],
                table_ref[start : start + depth, across],
                preferred_element_type=jnp.float32,
            )
        req[:, across] = (out[:rows] + out[3 * rows :]) * inverse_temperature
        pas[:, across] = (out[rows : 2 * rows] + out[2 * rows : 3 * rows]) * inverse_temperature
        for which, (src, dst) in enumerate(((req, req_hbm), (pas, pas_hbm))):
            copy = pltpu.make_async_copy(
                src.at[:, across], dst.at[:, across], sem.at[2 * piece + which]
            )
            copy.start()
            copies.append(copy)
    for copy in copies:
        copy.wait()


def on_device(queries, documents, positive, hard_ids):
    n = lax.axis_size("row")
    rows, width = queries.shape
    total = 2 * rows * n
    vmem = pl.BlockSpec(memory_space=pltpu.VMEM)
    anywhere = pl.BlockSpec(memory_space=pl.ANY)
    inputs = (queries, documents, positive, hard_ids)
    table, left, losses = pl.pallas_call(
        functools.partial(kernel, n),
        out_shape=(
            pltpu.VMEM((total, width + total), jnp.bfloat16),
            pltpu.VMEM((4 * rows, total), jnp.bfloat16),
            pltpu.VMEM((1, LANES), jnp.float32),
        ),
        in_specs=[anywhere] * 4,
        out_specs=(vmem, vmem, vmem),
        scratch_shapes=[
            pltpu.VMEM((rows, width), jnp.float32),
            pltpu.VMEM((rows, width), jnp.float32),
            pltpu.SMEM((rows,), jnp.int32),
            pltpu.VMEM(hard_ids.shape, jnp.int32),
            pltpu.VMEM((total, total), jnp.float32),
            pltpu.VMEM((total, total), jnp.float32),
            pltpu.VMEM((LANES, LANES), jnp.float32),
            pltpu.SemaphoreType.DMA((4,)),
            pltpu.SemaphoreType.DMA((n // 2, 2)),
            pltpu.SemaphoreType.DMA((n // 2, 2)),
            pltpu.SemaphoreType.DMA((n // 2, 2)),
            pltpu.SemaphoreType.DMA((n, 2)),
            pltpu.SemaphoreType.DMA((2,)),
        ],
        compiler_params=pltpu.CompilerParams(
            collective_id=0,
            has_side_effects=True,
            vmem_limit_bytes=8 * total * total + 6 * 1024 * 1024,
        ),
    )(*(pltpu.with_memory_space_constraint(a, pltpu.HBM) for a in inputs))
    table, left, losses = (
        pltpu.with_memory_space_constraint(a, pltpu.VMEM) for a in (table, left, losses)
    )
    request, passage, losses = pl.pallas_call(
        functools.partial(finish, width),
        out_shape=(
            jax.ShapeDtypeStruct((rows, width), jnp.float32),
            jax.ShapeDtypeStruct((rows, width), jnp.float32),
            jax.ShapeDtypeStruct((1, rows), jnp.float32),
        ),
        in_specs=[vmem] * 3,
        out_specs=(anywhere,) * 3,
        scratch_shapes=[
            pltpu.VMEM((rows, width), jnp.float32),
            pltpu.VMEM((rows, width), jnp.float32),
            pltpu.VMEM((1, rows), jnp.float32),
            pltpu.SemaphoreType.DMA((2 * PIECES + 1,)),
        ],
        compiler_params=pltpu.CompilerParams(vmem_limit_bytes=6 * 1024 * 1024),
    )(left, table, losses)
    return request, passage, losses.reshape(rows)


def solution(mesh):
    return jax.shard_map(
        on_device,
        mesh=mesh,
        in_specs=(
            P(("groups", "row"), "col"),
            P(("groups", "row"), "col"),
            P(("groups", "row")),
            P(("groups", "row"), None),
        ),
        out_specs=(P(("groups", "row"), "col"), P(("groups", "row"), "col"), P(("groups", "row"))),
        check_vma=False,
    )
```

```python
import functools

import jax
import jax.numpy as jnp
from jax import lax
from jax.experimental import pallas as pl
from jax.experimental.pallas import tpu as pltpu
from jax.sharding import PartitionSpec as P

inverse_temperature = 20.0
hardness_multiplier = 3.0
MESH = pl.DeviceIdType.MESH
LANES = 128
PIECES = 2


def repeat(count, body):
    if count <= 8:
        for step in range(count):
            body(step)
    else:
        lax.fori_loop(0, count, lambda step, carry: (body(step), carry)[1], 0)


def kernel(
    n,
    q_hbm,
    d_hbm,
    pos_hbm,
    hid_hbm,
    table,
    left_ref,
    loss_ref,
    q_in,
    d_in,
    pos_in,
    hid_in,
    scores,
    landed,
    flipped,
    in_sem,
    up_sem,
    down_sem,
    side_sem,
    recv_sem,
    col_sem,
):
    rows, width = q_in.shape
    pair_rows = 2 * rows
    total = pair_rows * n
    chunks = total // LANES
    per_chunk = LANES // pair_rows
    me = lax.axis_index("row")
    core = lax.axis_index("col")
    depth = n // 2
    z, x = me // 2, me % 2
    twin = z * 2 + (1 - x)

    def line(place):
        return place * 2 + x

    loads = [
        pltpu.make_async_copy(src, dst, in_sem.at[i])
        for i, (src, dst) in enumerate(
            ((pos_hbm, pos_in), (q_hbm, q_in), (d_hbm, d_in), (hid_hbm, hid_in))
        )
    ]
    for load in loads:
        load.start()

    barrier = pltpu.get_barrier_semaphore()

    def greet(device):
        pl.semaphore_signal(barrier, inc=1, device_id=device, device_id_type=MESH)

    greet({"row": twin})
    greet({"col": 1 - core})

    def greet_line(step):
        high, low = z + step + 1, z - step - 1
        pl.when(high < depth)(lambda: greet({"row": line(high)}))
        pl.when(low >= 0)(lambda: greet({"row": line(low)}))

    repeat(depth - 1, greet_line)

    for load in loads:
        load.wait()

    places = [pos_in[i] - me * rows for i in range(rows)]

    def to_documents(value):
        at = lax.broadcasted_iota(jnp.int32, value.shape, 0)
        out = jnp.zeros_like(value)
        for i in range(rows):
            out = jnp.where(at == places[i], value[i : i + 1, :], out)
        return out

    def to_queries(value):
        at = lax.broadcasted_iota(jnp.int32, value.shape, 0)
        place = jnp.zeros(value.shape, jnp.int32)
        for i in range(rows):
            place = jnp.where(at == i, places[i], place)
        out = jnp.zeros_like(value)
        for t in range(rows):
            out = jnp.where(place == t, value[t : t + 1, :], out)
        return out

    mine = pl.ds(pl.multiple_of(me * pair_rows, pair_rows), pair_rows)
    queries = to_documents(q_in[...])
    documents = d_in[...]
    lane = lax.broadcasted_iota(jnp.int32, (rows, total), 1)
    within = lane & (pair_rows - 1)
    document_id = jnp.where(
        within >= rows, (lane - within) // 2 + within - rows, -1
    )
    hard = hid_in[...]
    tally = jnp.zeros((rows, total), jnp.float32)
    for k in range(hard.shape[1]):
        tally = tally + jnp.where(hard[:, k : k + 1] == document_id, 1.0, 0.0)
    table[mine, :width] = jnp.concatenate([queries, documents], axis=0).astype(jnp.bfloat16)
    table[mine, width:] = jnp.concatenate(
        [to_documents(tally), jnp.zeros_like(tally)], axis=0
    ).astype(jnp.bfloat16)

    pl.semaphore_wait(barrier, depth + 1)

    halves = (pl.ds(0, width // 2), pl.ds(width // 2, width // 2 + total))

    def block_copy(source, half, target, sem):
        block = table.at[
            pl.ds(pl.multiple_of(source * pair_rows, pair_rows), pair_rows), halves[half]
        ]
        return pltpu.make_async_remote_copy(
            src_ref=block,
            dst_ref=block,
            send_sem=sem,
            recv_sem=recv_sem.at[source, half],
            device_id={"row": target},
            device_id_type=MESH,
        )

    def upward(far, half):
        return block_copy(me, half, line(z + far), up_sem.at[far, half])

    def downward(far, half):
        return block_copy(me, half, line(z - far), down_sem.at[far, half])

    def along(far, act):
        for half in range(2):
            pl.when(z + far < depth)(lambda: act(upward(far, half)))
            pl.when(z - far >= 0)(lambda: act(downward(far, half)))

    def sideward(place, half):
        return block_copy(line(place), half, twin, side_sem.at[place, half])

    def arrival(source, half):
        block_copy(source, half, twin, side_sem.at[0, half]).wait_recv()

    for half in range(2):
        sideward(z, half).start()
    repeat(depth - 1, lambda step: along(step + 1, lambda copy: copy.start()))

    def relay(step):
        low, high = z - step - 1, z + step + 1
        for half in range(2):

            @pl.when(low >= 0)
            def _():
                arrival(line(low), half)
                sideward(low, half).start()

            @pl.when(high < depth)
            def _():
                arrival(line(high), half)
                sideward(high, half).start()

    repeat(depth - 1, relay)

    def part(c):
        start = c * LANES
        return pl.ds(start if isinstance(c, int) else pl.multiple_of(start, LANES), LANES)

    for half in range(2):
        repeat(depth, lambda place: arrival(place * 2 + 1 - x, half))
        features = slice(half * width // 2, (half + 1) * width // 2)

        def multiply(c):
            def against(e):
                product = lax.dot_general(
                    table[part(c), features],
                    table[part(e), features],
                    (((1,), (1,)), ((), ())),
                    preferred_element_type=jnp.float32,
                )
                if half == 1:
                    product = product + scores[part(c), part(e)]
                scores[part(c), part(e)] = product

            repeat(chunks, against)

        repeat(chunks, multiply)

    exchange = pltpu.make_async_remote_copy(
        src_ref=scores,
        dst_ref=landed,
        send_sem=col_sem.at[0],
        recv_sem=col_sem.at[1],
        device_id={"col": 1 - core},
        device_id_type=MESH,
    )
    exchange.start()

    half = (per_chunk, rows, total)
    column = lax.broadcasted_iota(jnp.int32, half, 2)
    is_document = (column & rows) != 0
    own_column = (
        lax.broadcasted_iota(jnp.int32, half, 0) * pair_rows
        + lax.broadcasted_iota(jnp.int32, half, 1)
        + rows
    )

    def bias_of(c):
        counts = table[part(c), width:].astype(jnp.float32)
        counts = counts.reshape(per_chunk, pair_rows, total)[:, :rows]
        return jnp.log(1.0 + hardness_multiplier * counts)

    tile = (rows, LANES)
    tile_row = lax.broadcasted_iota(jnp.int32, tile, 0)
    tile_lane = lax.broadcasted_iota(jnp.int32, tile, 1)
    across_place = jnp.full(tile, -1, jnp.int32)
    down_place = jnp.zeros(tile, jnp.int32)
    for i in range(rows):
        across_place = jnp.where(tile_lane == i, places[i], across_place)
        down_place = jnp.where(tile_row == i, places[i], down_place)

    def anchor_rows(c):
        at = tile_lane + c * LANES - (me * pair_rows + rows)
        return jnp.where(at == down_place, -1.0, 0.0)

    early = bias_of(0) if chunks == 1 else None
    exchange.wait()

    def weigh(c):
        bias = early if chunks == 1 else bias_of(c)
        logits = (scores[part(c), :] + landed[part(c), :]) * inverse_temperature
        logits = logits.reshape(per_chunk, pair_rows, total)
        is_positive = column == own_column + c * LANES
        query_logits = jnp.where(is_document, logits[:, :rows] + bias, -jnp.inf)
        doc_logits = jnp.where(
            is_document & jnp.logical_not(is_positive), logits[:, rows:], -jnp.inf
        )
        peak = jnp.max(jnp.maximum(query_logits, doc_logits), axis=2, keepdims=True)
        query_terms, doc_terms = jnp.exp(query_logits - peak), jnp.exp(doc_logits - peak)
        mass = jnp.sum(query_terms + doc_terms, axis=2, keepdims=True)
        lse = peak + jnp.log(mass)
        share = 1.0 / mass
        losses = lse - jnp.sum(jnp.where(is_positive, query_logits, 0.0), axis=2, keepdims=True)
        weights = jnp.concatenate(
            [query_terms * share, doc_terms * share], axis=1
        )
        scores[part(c), :] = weights.reshape(LANES, total)
        landed[part(c), :LANES] = jnp.broadcast_to(
            jnp.concatenate([losses, losses], axis=1), (per_chunk, pair_rows, LANES)
        ).reshape(LANES, LANES)

    repeat(chunks, weigh)

    upper = pl.ds(pl.multiple_of(me * pair_rows, rows), rows)
    lower = pl.ds(pl.multiple_of(me * pair_rows + rows, rows), rows)
    sublane = lax.broadcasted_iota(jnp.int32, (rows, total), 0)
    heads = jnp.where(lane == me * pair_rows + sublane, -1.0, scores[lower, :])
    left_ref[: 2 * rows, :] = jnp.concatenate(
        [to_queries(scores[upper, :]), heads], axis=0
    ).astype(jnp.bfloat16)
    own_tile = pl.ds(pl.multiple_of(me // per_chunk * LANES, LANES), LANES)
    own_rows = pl.ds(
        pl.multiple_of(lax.rem(me, per_chunk) * pair_rows + rows, rows), rows
    )

    def columns(c):
        flipped[...] = scores[part(c), own_tile].T
        left_ref[2 * rows :, part(c)] = jnp.concatenate(
            [flipped[own_rows, :], anchor_rows(c)], axis=0
        ).astype(jnp.bfloat16)

    repeat(chunks, columns)

    losses = landed[upper, :LANES]
    at = lax.broadcasted_iota(jnp.int32, losses.shape, 0)
    loss_ref[...] = jnp.sum(jnp.where(across_place == at, losses, 0.0), axis=0, keepdims=True)

    def drain(place):
        for half in range(2):
            sideward(place, half).wait_send()

    repeat(depth, drain)
    repeat(depth - 1, lambda step: along(step + 1, lambda copy: copy.wait_send()))


def finish(width, left_ref, table_ref, loss_in, req_hbm, pas_hbm, loss_hbm, req, pas, loss, sem):
    rows = req.shape[0]
    loss[...] = loss_in[:, :rows]
    loss_copy = pltpu.make_async_copy(loss, loss_hbm, sem.at[2 * PIECES])
    loss_copy.start()
    total = left_ref.shape[1]
    step = width // PIECES
    copies = [loss_copy]
    for piece in range(PIECES):
        across = pl.ds(piece * step, step)
        out = jnp.zeros((4 * rows, step), jnp.float32)
        for start in range(0, total, LANES):
            depth = min(total, LANES)
            out = out + jnp.dot(
                left_ref[:, start : start + depth],
                table_ref[start : start + depth, across],
                preferred_element_type=jnp.float32,
            )
        req[:, across] = (out[:rows] + out[3 * rows :]) * inverse_temperature
        pas[:, across] = (out[rows : 2 * rows] + out[2 * rows : 3 * rows]) * inverse_temperature
        for which, (src, dst) in enumerate(((req, req_hbm), (pas, pas_hbm))):
            copy = pltpu.make_async_copy(
                src.at[:, across], dst.at[:, across], sem.at[2 * piece + which]
            )
            copy.start()
            copies.append(copy)
    for copy in copies:
        copy.wait()


def on_device(queries, documents, positive, hard_ids):
    n = lax.axis_size("row")
    rows, width = queries.shape
    total = 2 * rows * n
    vmem = pl.BlockSpec(memory_space=pltpu.VMEM)
    anywhere = pl.BlockSpec(memory_space=pl.ANY)
    inputs = (queries, documents, positive, hard_ids)
    table, left, losses = pl.pallas_call(
        functools.partial(kernel, n),
        out_shape=(
            pltpu.VMEM((total, width + total), jnp.bfloat16),
            pltpu.VMEM((4 * rows, total), jnp.bfloat16),
            pltpu.VMEM((1, LANES), jnp.float32),
        ),
        in_specs=[anywhere] * 4,
        out_specs=(vmem, vmem, vmem),
        scratch_shapes=[
            pltpu.VMEM((rows, width), jnp.float32),
            pltpu.VMEM((rows, width), jnp.float32),
            pltpu.SMEM((rows,), jnp.int32),
            pltpu.VMEM(hard_ids.shape, jnp.int32),
            pltpu.VMEM((total, total), jnp.float32),
            pltpu.VMEM((total, total), jnp.float32),
            pltpu.VMEM((LANES, LANES), jnp.float32),
            pltpu.SemaphoreType.DMA((4,)),
            pltpu.SemaphoreType.DMA((n // 2, 2)),
            pltpu.SemaphoreType.DMA((n // 2, 2)),
            pltpu.SemaphoreType.DMA((n // 2, 2)),
            pltpu.SemaphoreType.DMA((n, 2)),
            pltpu.SemaphoreType.DMA((2,)),
        ],
        compiler_params=pltpu.CompilerParams(
            collective_id=0,
            has_side_effects=True,
            vmem_limit_bytes=8 * total * total + 6 * 1024 * 1024,
        ),
    )(*(pltpu.with_memory_space_constraint(a, pltpu.HBM) for a in inputs))
    table, left, losses = (
        pltpu.with_memory_space_constraint(a, pltpu.VMEM) for a in (table, left, losses)
    )
    request, passage, losses = pl.pallas_call(
        functools.partial(finish, width),
        out_shape=(
            jax.ShapeDtypeStruct((rows, width), jnp.float32),
            jax.ShapeDtypeStruct((rows, width), jnp.float32),
            jax.ShapeDtypeStruct((1, rows), jnp.float32),
        ),
        in_specs=[vmem] * 3,
        out_specs=(anywhere,) * 3,
        scratch_shapes=[
            pltpu.VMEM((rows, width), jnp.float32),
            pltpu.VMEM((rows, width), jnp.float32),
            pltpu.VMEM((1, rows), jnp.float32),
            pltpu.SemaphoreType.DMA((2 * PIECES + 1,)),
        ],
        compiler_params=pltpu.CompilerParams(vmem_limit_bytes=6 * 1024 * 1024),
    )(left, table, losses)
    return request, passage, losses.reshape(rows)


def solution(mesh):
    return jax.shard_map(
        on_device,
        mesh=mesh,
        in_specs=(
            P(("groups", "row"), "col"),
            P(("groups", "row"), "col"),
            P(("groups", "row")),
            P(("groups", "row"), None),
        ),
        out_specs=(P(("groups", "row"), "col"), P(("groups", "row"), "col"), P(("groups", "row"))),
        check_vma=False,
    )
```

```python
import functools

import jax
import jax.numpy as jnp
from jax import lax
from jax.experimental import pallas as pl
from jax.experimental.pallas import tpu as pltpu
from jax.sharding import PartitionSpec as P

inverse_temperature = 20.0
hardness_multiplier = 3.0
MESH = pl.DeviceIdType.MESH
LANES = 128
PIECES = 2
SHARES = 1


def repeat(count, body):
    if count <= 8:
        for step in range(count):
            body(step)
    else:
        lax.fori_loop(0, count, lambda step, carry: (body(step), carry)[1], 0)


def kernel(
    n,
    q_hbm,
    d_hbm,
    pos_hbm,
    hid_hbm,
    table,
    left_ref,
    loss_ref,
    q_in,
    d_in,
    pos_in,
    hid_in,
    scores,
    landed,
    flipped,
    in_sem,
    up_sem,
    down_sem,
    side_sem,
    recv_sem,
    col_sem,
):
    rows, width = q_in.shape
    pair_rows = 2 * rows
    total = pair_rows * n
    chunks = total // LANES
    per_chunk = LANES // pair_rows
    me = lax.axis_index("row")
    core = lax.axis_index("col")
    depth = n // 2
    z, x = me // 2, me % 2
    twin = z * 2 + (1 - x)

    def line(place):
        return place * 2 + x

    loads = [
        pltpu.make_async_copy(src, dst, in_sem.at[i])
        for i, (src, dst) in enumerate(
            ((pos_hbm, pos_in), (q_hbm, q_in), (d_hbm, d_in), (hid_hbm, hid_in))
        )
    ]
    for load in loads:
        load.start()

    barrier = pltpu.get_barrier_semaphore()

    def greet(device):
        pl.semaphore_signal(barrier, inc=1, device_id=device, device_id_type=MESH)

    greet({"row": twin})
    greet({"col": 1 - core})

    def greet_line(step):
        high, low = z + step + 1, z - step - 1
        pl.when(high < depth)(lambda: greet({"row": line(high)}))
        pl.when(low >= 0)(lambda: greet({"row": line(low)}))

    repeat(depth - 1, greet_line)

    for load in loads:
        load.wait()

    places = [pos_in[i] - me * rows for i in range(rows)]

    def to_documents(value):
        at = lax.broadcasted_iota(jnp.int32, value.shape, 0)
        out = jnp.zeros_like(value)
        for i in range(rows):
            out = jnp.where(at == places[i], value[i : i + 1, :], out)
        return out

    def to_queries(value):
        at = lax.broadcasted_iota(jnp.int32, value.shape, 0)
        place = jnp.zeros(value.shape, jnp.int32)
        for i in range(rows):
            place = jnp.where(at == i, places[i], place)
        out = jnp.zeros_like(value)
        for t in range(rows):
            out = jnp.where(place == t, value[t : t + 1, :], out)
        return out

    mine = pl.ds(pl.multiple_of(me * pair_rows, pair_rows), pair_rows)
    queries = to_documents(q_in[...])
    documents = d_in[...]
    lane = lax.broadcasted_iota(jnp.int32, (rows, total), 1)
    within = lane & (pair_rows - 1)
    document_id = jnp.where(
        within >= rows, (lane - within) // 2 + within - rows, -1
    )
    hard = hid_in[...]
    tally = jnp.zeros((rows, total), jnp.float32)
    for k in range(hard.shape[1]):
        tally = tally + jnp.where(hard[:, k : k + 1] == document_id, 1.0, 0.0)
    table[mine, :width] = jnp.concatenate([queries, documents], axis=0).astype(jnp.bfloat16)
    table[mine, width:] = jnp.concatenate(
        [to_documents(tally), jnp.zeros_like(tally)], axis=0
    ).astype(jnp.bfloat16)

    pl.semaphore_wait(barrier, depth + 1)

    halves = (pl.ds(0, width + total),)

    def block_copy(source, half, target, sem):
        block = table.at[
            pl.ds(pl.multiple_of(source * pair_rows, pair_rows), pair_rows), halves[half]
        ]
        return pltpu.make_async_remote_copy(
            src_ref=block,
            dst_ref=block,
            send_sem=sem,
            recv_sem=recv_sem.at[source, half],
            device_id={"row": target},
            device_id_type=MESH,
        )

    def upward(far, half):
        return block_copy(me, half, line(z + far), up_sem.at[far, half])

    def downward(far, half):
        return block_copy(me, half, line(z - far), down_sem.at[far, half])

    def along(far, act):
        for half in range(SHARES):
            pl.when(z + far < depth)(lambda: act(upward(far, half)))
            pl.when(z - far >= 0)(lambda: act(downward(far, half)))

    def sideward(place, half):
        return block_copy(line(place), half, twin, side_sem.at[place, half])

    def arrival(source, half):
        block_copy(source, half, twin, side_sem.at[0, half]).wait_recv()

    for half in range(SHARES):
        sideward(z, half).start()
    repeat(depth - 1, lambda step: along(step + 1, lambda copy: copy.start()))

    def relay(step):
        low, high = z - step - 1, z + step + 1
        for half in range(SHARES):

            @pl.when(low >= 0)
            def _():
                arrival(line(low), half)
                sideward(low, half).start()

            @pl.when(high < depth)
            def _():
                arrival(line(high), half)
                sideward(high, half).start()

    repeat(depth - 1, relay)

    def part(c):
        start = c * LANES
        return pl.ds(start if isinstance(c, int) else pl.multiple_of(start, LANES), LANES)

    for half in range(SHARES):
        repeat(depth, lambda place: arrival(place * 2 + 1 - x, half))
        features = slice(half * width // SHARES, (half + 1) * width // SHARES)

        def multiply(c):
            def against(e):
                product = lax.dot_general(
                    table[part(c), features],
                    table[part(e), features],
                    (((1,), (1,)), ((), ())),
                    preferred_element_type=jnp.float32,
                )
                if half > 0:
                    product = product + scores[part(c), part(e)]
                scores[part(c), part(e)] = product

            repeat(chunks, against)

        repeat(chunks, multiply)

    exchange = pltpu.make_async_remote_copy(
        src_ref=scores,
        dst_ref=landed,
        send_sem=col_sem.at[0],
        recv_sem=col_sem.at[1],
        device_id={"col": 1 - core},
        device_id_type=MESH,
    )
    exchange.start()

    half = (per_chunk, rows, total)
    column = lax.broadcasted_iota(jnp.int32, half, 2)
    is_document = (column & rows) != 0
    own_column = (
        lax.broadcasted_iota(jnp.int32, half, 0) * pair_rows
        + lax.broadcasted_iota(jnp.int32, half, 1)
        + rows
    )

    def bias_of(c):
        counts = table[part(c), width:].astype(jnp.float32)
        counts = counts.reshape(per_chunk, pair_rows, total)[:, :rows]
        return jnp.log(1.0 + hardness_multiplier * counts)

    tile = (rows, LANES)
    tile_row = lax.broadcasted_iota(jnp.int32, tile, 0)
    tile_lane = lax.broadcasted_iota(jnp.int32, tile, 1)
    across_place = jnp.full(tile, -1, jnp.int32)
    down_place = jnp.zeros(tile, jnp.int32)
    for i in range(rows):
        across_place = jnp.where(tile_lane == i, places[i], across_place)
        down_place = jnp.where(tile_row == i, places[i], down_place)

    def anchor_rows(c):
        at = tile_lane + c * LANES - (me * pair_rows + rows)
        return jnp.where(at == down_place, -1.0, 0.0)

    early = bias_of(0) if chunks == 1 else None
    exchange.wait()

    def weigh(c):
        bias = early if chunks == 1 else bias_of(c)
        logits = (scores[part(c), :] + landed[part(c), :]) * inverse_temperature
        logits = logits.reshape(per_chunk, pair_rows, total)
        is_positive = column == own_column + c * LANES
        query_logits = jnp.where(is_document, logits[:, :rows] + bias, -jnp.inf)
        doc_logits = jnp.where(
            is_document & jnp.logical_not(is_positive), logits[:, rows:], -jnp.inf
        )
        peak = jnp.max(jnp.maximum(query_logits, doc_logits), axis=2, keepdims=True)
        query_terms, doc_terms = jnp.exp(query_logits - peak), jnp.exp(doc_logits - peak)
        mass = jnp.sum(query_terms + doc_terms, axis=2, keepdims=True)
        lse = peak + jnp.log(mass)
        share = 1.0 / mass
        losses = lse - jnp.sum(jnp.where(is_positive, query_logits, 0.0), axis=2, keepdims=True)
        weights = jnp.concatenate(
            [query_terms * share, doc_terms * share], axis=1
        )
        scores[part(c), :] = weights.reshape(LANES, total)
        landed[part(c), :LANES] = jnp.broadcast_to(
            jnp.concatenate([losses, losses], axis=1), (per_chunk, pair_rows, LANES)
        ).reshape(LANES, LANES)

    repeat(chunks, weigh)

    upper = pl.ds(pl.multiple_of(me * pair_rows, rows), rows)
    lower = pl.ds(pl.multiple_of(me * pair_rows + rows, rows), rows)
    sublane = lax.broadcasted_iota(jnp.int32, (rows, total), 0)
    heads = jnp.where(lane == me * pair_rows + sublane, -1.0, scores[lower, :])
    left_ref[: 2 * rows, :] = jnp.concatenate(
        [to_queries(scores[upper, :]), heads], axis=0
    ).astype(jnp.bfloat16)
    own_tile = pl.ds(pl.multiple_of(me // per_chunk * LANES, LANES), LANES)
    own_rows = pl.ds(
        pl.multiple_of(lax.rem(me, per_chunk) * pair_rows + rows, rows), rows
    )

    def columns(c):
        flipped[...] = scores[part(c), own_tile].T
        left_ref[2 * rows :, part(c)] = jnp.concatenate(
            [flipped[own_rows, :], anchor_rows(c)], axis=0
        ).astype(jnp.bfloat16)

    repeat(chunks, columns)

    losses = landed[upper, :LANES]
    at = lax.broadcasted_iota(jnp.int32, losses.shape, 0)
    loss_ref[...] = jnp.sum(jnp.where(across_place == at, losses, 0.0), axis=0, keepdims=True)

    def drain(place):
        for half in range(SHARES):
            sideward(place, half).wait_send()

    repeat(depth, drain)
    repeat(depth - 1, lambda step: along(step + 1, lambda copy: copy.wait_send()))


def finish(width, left_ref, table_ref, loss_in, req_hbm, pas_hbm, loss_hbm, req, pas, loss, sem):
    rows = req.shape[0]
    loss[...] = loss_in[:, :rows]
    loss_copy = pltpu.make_async_copy(loss, loss_hbm, sem.at[2 * PIECES])
    loss_copy.start()
    total = left_ref.shape[1]
    step = width // PIECES
    copies = [loss_copy]
    for piece in range(PIECES):
        across = pl.ds(piece * step, step)
        out = jnp.zeros((4 * rows, step), jnp.float32)
        for start in range(0, total, LANES):
            depth = min(total, LANES)
            out = out + jnp.dot(
                left_ref[:, start : start + depth],
                table_ref[start : start + depth, across],
                preferred_element_type=jnp.float32,
            )
        req[:, across] = (out[:rows] + out[3 * rows :]) * inverse_temperature
        pas[:, across] = (out[rows : 2 * rows] + out[2 * rows : 3 * rows]) * inverse_temperature
        for which, (src, dst) in enumerate(((req, req_hbm), (pas, pas_hbm))):
            copy = pltpu.make_async_copy(
                src.at[:, across], dst.at[:, across], sem.at[2 * piece + which]
            )
            copy.start()
            copies.append(copy)
    for copy in copies:
        copy.wait()


def on_device(queries, documents, positive, hard_ids):
    n = lax.axis_size("row")
    rows, width = queries.shape
    total = 2 * rows * n
    vmem = pl.BlockSpec(memory_space=pltpu.VMEM)
    anywhere = pl.BlockSpec(memory_space=pl.ANY)
    inputs = (queries, documents, positive, hard_ids)
    table, left, losses = pl.pallas_call(
        functools.partial(kernel, n),
        out_shape=(
            pltpu.VMEM((total, width + total), jnp.bfloat16),
            pltpu.VMEM((4 * rows, total), jnp.bfloat16),
            pltpu.VMEM((1, LANES), jnp.float32),
        ),
        in_specs=[anywhere] * 4,
        out_specs=(vmem, vmem, vmem),
        scratch_shapes=[
            pltpu.VMEM((rows, width), jnp.float32),
            pltpu.VMEM((rows, width), jnp.float32),
            pltpu.SMEM((rows,), jnp.int32),
            pltpu.VMEM(hard_ids.shape, jnp.int32),
            pltpu.VMEM((total, total), jnp.float32),
            pltpu.VMEM((total, total), jnp.float32),
            pltpu.VMEM((LANES, LANES), jnp.float32),
            pltpu.SemaphoreType.DMA((4,)),
            pltpu.SemaphoreType.DMA((n // 2, SHARES)),
            pltpu.SemaphoreType.DMA((n // 2, SHARES)),
            pltpu.SemaphoreType.DMA((n // 2, SHARES)),
            pltpu.SemaphoreType.DMA((n, SHARES)),
            pltpu.SemaphoreType.DMA((2,)),
        ],
        compiler_params=pltpu.CompilerParams(
            collective_id=0,
            has_side_effects=True,
            vmem_limit_bytes=8 * total * total + 6 * 1024 * 1024,
        ),
    )(*(pltpu.with_memory_space_constraint(a, pltpu.HBM) for a in inputs))
    table, left, losses = (
        pltpu.with_memory_space_constraint(a, pltpu.VMEM) for a in (table, left, losses)
    )
    request, passage, losses = pl.pallas_call(
        functools.partial(finish, width),
        out_shape=(
            jax.ShapeDtypeStruct((rows, width), jnp.float32),
            jax.ShapeDtypeStruct((rows, width), jnp.float32),
            jax.ShapeDtypeStruct((1, rows), jnp.float32),
        ),
        in_specs=[vmem] * 3,
        out_specs=(anywhere,) * 3,
        scratch_shapes=[
            pltpu.VMEM((rows, width), jnp.float32),
            pltpu.VMEM((rows, width), jnp.float32),
            pltpu.VMEM((1, rows), jnp.float32),
            pltpu.SemaphoreType.DMA((2 * PIECES + 1,)),
        ],
        compiler_params=pltpu.CompilerParams(vmem_limit_bytes=6 * 1024 * 1024),
    )(left, table, losses)
    return request, passage, losses.reshape(rows)


def solution(mesh):
    return jax.shard_map(
        on_device,
        mesh=mesh,
        in_specs=(
            P(("groups", "row"), "col"),
            P(("groups", "row"), "col"),
            P(("groups", "row")),
            P(("groups", "row"), None),
        ),
        out_specs=(P(("groups", "row"), "col"), P(("groups", "row"), "col"), P(("groups", "row"))),
        check_vma=False,
    )
```

```python
import functools

import jax
import jax.numpy as jnp
from jax import lax
from jax.experimental import pallas as pl
from jax.experimental.pallas import tpu as pltpu
from jax.sharding import PartitionSpec as P

inverse_temperature = 20.0
hardness_multiplier = 3.0
MESH = pl.DeviceIdType.MESH
LANES = 128
PIECES = 2


def repeat(count, body):
    if count <= 8:
        for step in range(count):
            body(step)
    else:
        lax.fori_loop(0, count, lambda step, carry: (body(step), carry)[1], 0)


def kernel(
    n,
    q_hbm,
    d_hbm,
    pos_hbm,
    hid_hbm,
    table,
    left_ref,
    loss_ref,
    q_in,
    d_in,
    pos_in,
    hid_in,
    scores,
    landed,
    flipped,
    in_sem,
    send_sem,
    recv_sem,
    col_sem,
):
    rows, width = q_in.shape
    pair_rows = 2 * rows
    total = pair_rows * n
    chunks = total // LANES
    per_chunk = LANES // pair_rows
    me = lax.axis_index("row")
    core = lax.axis_index("col")

    def peer(step):
        return lax.rem(me + step + 1, n)

    def source(step):
        return lax.rem(me + n - step - 1, n)

    loads = [
        pltpu.make_async_copy(src, dst, in_sem.at[i])
        for i, (src, dst) in enumerate(
            ((pos_hbm, pos_in), (q_hbm, q_in), (d_hbm, d_in), (hid_hbm, hid_in))
        )
    ]
    for load in loads:
        load.start()

    barrier = pltpu.get_barrier_semaphore()

    def greet(device):
        pl.semaphore_signal(barrier, inc=1, device_id=device, device_id_type=MESH)

    greet({"col": 1 - core})
    repeat(n - 1, lambda step: greet({"row": peer(step)}))

    for load in loads:
        load.wait()

    places = [pos_in[i] - me * rows for i in range(rows)]

    def to_documents(value):
        at = lax.broadcasted_iota(jnp.int32, value.shape, 0)
        out = jnp.zeros_like(value)
        for i in range(rows):
            out = jnp.where(at == places[i], value[i : i + 1, :], out)
        return out

    def to_queries(value):
        at = lax.broadcasted_iota(jnp.int32, value.shape, 0)
        place = jnp.zeros(value.shape, jnp.int32)
        for i in range(rows):
            place = jnp.where(at == i, places[i], place)
        out = jnp.zeros_like(value)
        for t in range(rows):
            out = jnp.where(place == t, value[t : t + 1, :], out)
        return out

    mine = pl.ds(pl.multiple_of(me * pair_rows, pair_rows), pair_rows)
    queries = to_documents(q_in[...])
    documents = d_in[...]
    lane = lax.broadcasted_iota(jnp.int32, (rows, total), 1)
    within = lane & (pair_rows - 1)
    document_id = jnp.where(
        within >= rows, (lane - within) // 2 + within - rows, -1
    )
    hard = hid_in[...]
    tally = jnp.zeros((rows, total), jnp.float32)
    for k in range(hard.shape[1]):
        tally = tally + jnp.where(hard[:, k : k + 1] == document_id, 1.0, 0.0)
    table[mine, :width] = jnp.concatenate([queries, documents], axis=0).astype(jnp.bfloat16)
    table[mine, width:] = jnp.concatenate(
        [to_documents(tally), jnp.zeros_like(tally)], axis=0
    ).astype(jnp.bfloat16)

    pl.semaphore_wait(barrier, n)

    def block_copy(owner, target, slot):
        block = table.at[pl.ds(pl.multiple_of(owner * pair_rows, pair_rows), pair_rows)]
        return pltpu.make_async_remote_copy(
            src_ref=block,
            dst_ref=block,
            send_sem=send_sem.at[slot],
            recv_sem=recv_sem.at[owner],
            device_id={"row": target},
            device_id_type=MESH,
        )

    repeat(n - 1, lambda step: block_copy(me, peer(step), step).start())
    repeat(n - 1, lambda step: block_copy(source(step), peer(0), 0).wait_recv())

    def part(c):
        start = c * LANES
        return pl.ds(start if isinstance(c, int) else pl.multiple_of(start, LANES), LANES)

    def multiply(c):
        def against(e):
            scores[part(c), part(e)] = lax.dot_general(
                table[part(c), :width],
                table[part(e), :width],
                (((1,), (1,)), ((), ())),
                preferred_element_type=jnp.float32,
            )

        repeat(chunks, against)

    repeat(chunks, multiply)

    exchange = pltpu.make_async_remote_copy(
        src_ref=scores,
        dst_ref=landed,
        send_sem=col_sem.at[0],
        recv_sem=col_sem.at[1],
        device_id={"col": 1 - core},
        device_id_type=MESH,
    )
    exchange.start()

    half = (per_chunk, rows, total)
    column = lax.broadcasted_iota(jnp.int32, half, 2)
    is_document = (column & rows) != 0
    own_column = (
        lax.broadcasted_iota(jnp.int32, half, 0) * pair_rows
        + lax.broadcasted_iota(jnp.int32, half, 1)
        + rows
    )

    def bias_of(c):
        counts = table[part(c), width:].astype(jnp.float32)
        counts = counts.reshape(per_chunk, pair_rows, total)[:, :rows]
        return jnp.log(1.0 + hardness_multiplier * counts)

    tile = (rows, LANES)
    tile_row = lax.broadcasted_iota(jnp.int32, tile, 0)
    tile_lane = lax.broadcasted_iota(jnp.int32, tile, 1)
    across_place = jnp.full(tile, -1, jnp.int32)
    down_place = jnp.zeros(tile, jnp.int32)
    for i in range(rows):
        across_place = jnp.where(tile_lane == i, places[i], across_place)
        down_place = jnp.where(tile_row == i, places[i], down_place)

    def anchor_rows(c):
        at = tile_lane + c * LANES - (me * pair_rows + rows)
        return jnp.where(at == down_place, -1.0, 0.0)

    early = bias_of(0) if chunks == 1 else None
    exchange.wait()

    def weigh(c):
        bias = early if chunks == 1 else bias_of(c)
        logits = (scores[part(c), :] + landed[part(c), :]) * inverse_temperature
        logits = logits.reshape(per_chunk, pair_rows, total)
        is_positive = column == own_column + c * LANES
        query_logits = jnp.where(is_document, logits[:, :rows] + bias, -jnp.inf)
        doc_logits = jnp.where(
            is_document & jnp.logical_not(is_positive), logits[:, rows:], -jnp.inf
        )
        peak = jnp.max(jnp.maximum(query_logits, doc_logits), axis=2, keepdims=True)
        query_terms, doc_terms = jnp.exp(query_logits - peak), jnp.exp(doc_logits - peak)
        mass = jnp.sum(query_terms + doc_terms, axis=2, keepdims=True)
        lse = peak + jnp.log(mass)
        share = 1.0 / mass
        losses = lse - jnp.sum(jnp.where(is_positive, query_logits, 0.0), axis=2, keepdims=True)
        weights = jnp.concatenate(
            [query_terms * share, doc_terms * share], axis=1
        )
        scores[part(c), :] = weights.reshape(LANES, total)
        landed[part(c), :LANES] = jnp.broadcast_to(
            jnp.concatenate([losses, losses], axis=1), (per_chunk, pair_rows, LANES)
        ).reshape(LANES, LANES)

    repeat(chunks, weigh)

    upper = pl.ds(pl.multiple_of(me * pair_rows, rows), rows)
    lower = pl.ds(pl.multiple_of(me * pair_rows + rows, rows), rows)
    sublane = lax.broadcasted_iota(jnp.int32, (rows, total), 0)
    heads = jnp.where(lane == me * pair_rows + sublane, -1.0, scores[lower, :])
    left_ref[: 2 * rows, :] = jnp.concatenate(
        [to_queries(scores[upper, :]), heads], axis=0
    ).astype(jnp.bfloat16)
    own_tile = pl.ds(pl.multiple_of(me // per_chunk * LANES, LANES), LANES)
    own_rows = pl.ds(
        pl.multiple_of(lax.rem(me, per_chunk) * pair_rows + rows, rows), rows
    )

    def columns(c):
        flipped[...] = scores[part(c), own_tile].T
        left_ref[2 * rows :, part(c)] = jnp.concatenate(
            [flipped[own_rows, :], anchor_rows(c)], axis=0
        ).astype(jnp.bfloat16)

    repeat(chunks, columns)

    losses = landed[upper, :LANES]
    at = lax.broadcasted_iota(jnp.int32, losses.shape, 0)
    loss_ref[...] = jnp.sum(jnp.where(across_place == at, losses, 0.0), axis=0, keepdims=True)

    repeat(n - 1, lambda step: block_copy(me, peer(step), step).wait_send())


def finish(width, left_ref, table_ref, loss_in, req_hbm, pas_hbm, loss_hbm, req, pas, loss, sem):
    rows = req.shape[0]
    loss[...] = loss_in[:, :rows]
    loss_copy = pltpu.make_async_copy(loss, loss_hbm, sem.at[2 * PIECES])
    loss_copy.start()
    total = left_ref.shape[1]
    step = width // PIECES
    copies = [loss_copy]
    for piece in range(PIECES):
        across = pl.ds(piece * step, step)
        out = jnp.zeros((4 * rows, step), jnp.float32)
        for start in range(0, total, LANES):
            depth = min(total, LANES)
            out = out + jnp.dot(
                left_ref[:, start : start + depth],
                table_ref[start : start + depth, across],
                preferred_element_type=jnp.float32,
            )
        req[:, across] = (out[:rows] + out[3 * rows :]) * inverse_temperature
        pas[:, across] = (out[rows : 2 * rows] + out[2 * rows : 3 * rows]) * inverse_temperature
        for which, (src, dst) in enumerate(((req, req_hbm), (pas, pas_hbm))):
            copy = pltpu.make_async_copy(
                src.at[:, across], dst.at[:, across], sem.at[2 * piece + which]
            )
            copy.start()
            copies.append(copy)
    for copy in copies:
        copy.wait()


def on_device(queries, documents, positive, hard_ids):
    n = lax.axis_size("row")
    rows, width = queries.shape
    total = 2 * rows * n
    vmem = pl.BlockSpec(memory_space=pltpu.VMEM)
    anywhere = pl.BlockSpec(memory_space=pl.ANY)
    inputs = (queries, documents, positive, hard_ids)
    table, left, losses = pl.pallas_call(
        functools.partial(kernel, n),
        out_shape=(
            pltpu.VMEM((total, width + total), jnp.bfloat16),
            pltpu.VMEM((4 * rows, total), jnp.bfloat16),
            pltpu.VMEM((1, LANES), jnp.float32),
        ),
        in_specs=[anywhere] * 4,
        out_specs=(vmem, vmem, vmem),
        scratch_shapes=[
            pltpu.VMEM((rows, width), jnp.float32),
            pltpu.VMEM((rows, width), jnp.float32),
            pltpu.SMEM((rows,), jnp.int32),
            pltpu.VMEM(hard_ids.shape, jnp.int32),
            pltpu.VMEM((total, total), jnp.float32),
            pltpu.VMEM((total, total), jnp.float32),
            pltpu.VMEM((LANES, LANES), jnp.float32),
            pltpu.SemaphoreType.DMA((4,)),
            pltpu.SemaphoreType.DMA((n - 1,)),
            pltpu.SemaphoreType.DMA((n,)),
            pltpu.SemaphoreType.DMA((2,)),
        ],
        compiler_params=pltpu.CompilerParams(
            collective_id=0,
            has_side_effects=True,
            vmem_limit_bytes=8 * total * total + 6 * 1024 * 1024,
        ),
    )(*(pltpu.with_memory_space_constraint(a, pltpu.HBM) for a in inputs))
    table, left, losses = (
        pltpu.with_memory_space_constraint(a, pltpu.VMEM) for a in (table, left, losses)
    )
    request, passage, losses = pl.pallas_call(
        functools.partial(finish, width),
        out_shape=(
            jax.ShapeDtypeStruct((rows, width), jnp.float32),
            jax.ShapeDtypeStruct((rows, width), jnp.float32),
            jax.ShapeDtypeStruct((1, rows), jnp.float32),
        ),
        in_specs=[vmem] * 3,
        out_specs=(anywhere,) * 3,
        scratch_shapes=[
            pltpu.VMEM((rows, width), jnp.float32),
            pltpu.VMEM((rows, width), jnp.float32),
            pltpu.VMEM((1, rows), jnp.float32),
            pltpu.SemaphoreType.DMA((2 * PIECES + 1,)),
        ],
        compiler_params=pltpu.CompilerParams(vmem_limit_bytes=6 * 1024 * 1024),
    )(left, table, losses)
    return request, passage, losses.reshape(rows)


def solution(mesh):
    return jax.shard_map(
        on_device,
        mesh=mesh,
        in_specs=(
            P(("groups", "row"), "col"),
            P(("groups", "row"), "col"),
            P(("groups", "row")),
            P(("groups", "row"), None),
        ),
        out_specs=(P(("groups", "row"), "col"), P(("groups", "row"), "col"), P(("groups", "row"))),
        check_vma=False,
    )
```

```python
import functools

import jax
import jax.numpy as jnp
from jax import lax
from jax.experimental import pallas as pl
from jax.experimental.pallas import tpu as pltpu
from jax.sharding import PartitionSpec as P

inverse_temperature = 20.0
hardness_multiplier = 3.0
MESH = pl.DeviceIdType.MESH
LANES = 128
PIECES = 2


def repeat(count, body):
    if count <= 8:
        for step in range(count):
            body(step)
    else:
        lax.fori_loop(0, count, lambda step, carry: (body(step), carry)[1], 0)


def kernel(
    n,
    q_hbm,
    d_hbm,
    pos_hbm,
    hid_hbm,
    table,
    left_ref,
    loss_ref,
    q_in,
    d_in,
    pos_in,
    hid_in,
    scores,
    landed,
    flipped,
    in_sem,
    send_sem,
    recv_sem,
    col_sem,
):
    rows, width = q_in.shape
    pair_rows = 2 * rows
    total = pair_rows * n
    chunks = total // LANES
    per_chunk = LANES // pair_rows
    me = lax.axis_index("row")
    core = lax.axis_index("col")
    depth = n // 2
    z, x = me // 2, me % 2
    twin = z * 2 + (1 - x)

    def line_peer(step):
        return lax.rem(z + step + 1, depth) * 2 + x

    def line_source(step):
        return lax.rem(z + depth - step - 1, depth) * 2 + x

    loads = [
        pltpu.make_async_copy(src, dst, in_sem.at[i])
        for i, (src, dst) in enumerate(
            ((pos_hbm, pos_in), (q_hbm, q_in), (d_hbm, d_in), (hid_hbm, hid_in))
        )
    ]
    for load in loads:
        load.start()

    barrier = pltpu.get_barrier_semaphore()

    def greet(step):
        pl.semaphore_signal(
            barrier, inc=1, device_id={"row": line_peer(step)}, device_id_type=MESH
        )

    repeat(depth - 1, greet)
    pl.semaphore_signal(barrier, inc=1, device_id={"row": twin}, device_id_type=MESH)
    pl.semaphore_signal(barrier, inc=1, device_id={"col": 1 - core}, device_id_type=MESH)

    for load in loads:
        load.wait()

    places = [pos_in[i] - me * rows for i in range(rows)]

    def to_documents(value):
        at = lax.broadcasted_iota(jnp.int32, value.shape, 0)
        out = jnp.zeros_like(value)
        for i in range(rows):
            out = jnp.where(at == places[i], value[i : i + 1, :], out)
        return out

    def to_queries(value):
        at = lax.broadcasted_iota(jnp.int32, value.shape, 0)
        place = jnp.zeros(value.shape, jnp.int32)
        for i in range(rows):
            place = jnp.where(at == i, places[i], place)
        out = jnp.zeros_like(value)
        for t in range(rows):
            out = jnp.where(place == t, value[t : t + 1, :], out)
        return out

    mine = pl.ds(pl.multiple_of(me * pair_rows, pair_rows), pair_rows)
    queries = to_documents(q_in[...])
    documents = d_in[...]
    lane = lax.broadcasted_iota(jnp.int32, (rows, total), 1)
    within = lane & (pair_rows - 1)
    document_id = jnp.where(
        within >= rows, (lane - within) // 2 + within - rows, -1
    )
    hard = hid_in[...]
    tally = jnp.zeros((rows, total), jnp.float32)
    for k in range(hard.shape[1]):
        tally = tally + jnp.where(hard[:, k : k + 1] == document_id, 1.0, 0.0)
    table[mine, :width] = jnp.concatenate([queries, documents], axis=0).astype(jnp.bfloat16)
    table[mine, width:] = jnp.concatenate(
        [to_documents(tally), jnp.zeros_like(tally)], axis=0
    ).astype(jnp.bfloat16)

    pl.semaphore_wait(barrier, depth + 1)

    def block_copy(source, target, slot):
        block = table.at[pl.ds(pl.multiple_of(source * pair_rows, pair_rows), pair_rows)]
        return pltpu.make_async_remote_copy(
            src_ref=block,
            dst_ref=block,
            send_sem=send_sem.at[slot],
            recv_sem=recv_sem.at[source],
            device_id={"row": target},
            device_id_type=MESH,
        )

    block_copy(me, twin, 0).start()
    repeat(depth - 1, lambda step: block_copy(me, line_peer(step), 1 + step).start())

    def forward(step):
        source = line_source(step)
        block_copy(source, twin, depth + step).wait_recv()
        block_copy(source, twin, depth + step).start()

    repeat(depth - 1, forward)
    block_copy(twin, twin, 0).wait_recv()
    repeat(
        depth - 1,
        lambda step: block_copy(line_source(step) + 1 - 2 * x, twin, 0).wait_recv(),
    )

    def part(c):
        start = c * LANES
        return pl.ds(start if isinstance(c, int) else pl.multiple_of(start, LANES), LANES)

    def multiply(c):
        def against(e):
            scores[part(c), part(e)] = lax.dot_general(
                table[part(c), :width],
                table[part(e), :width],
                (((1,), (1,)), ((), ())),
                preferred_element_type=jnp.float32,
            )

        repeat(chunks, against)

    repeat(chunks, multiply)

    exchange = pltpu.make_async_remote_copy(
        src_ref=scores,
        dst_ref=landed,
        send_sem=col_sem.at[0],
        recv_sem=col_sem.at[1],
        device_id={"col": 1 - core},
        device_id_type=MESH,
    )
    exchange.start()

    half = (per_chunk, rows, total)
    column = lax.broadcasted_iota(jnp.int32, half, 2)
    is_document = (column & rows) != 0
    own_column = (
        lax.broadcasted_iota(jnp.int32, half, 0) * pair_rows
        + lax.broadcasted_iota(jnp.int32, half, 1)
        + rows
    )

    def bias_of(c):
        counts = table[part(c), width:].astype(jnp.float32)
        counts = counts.reshape(per_chunk, pair_rows, total)[:, :rows]
        return jnp.log(1.0 + hardness_multiplier * counts)

    tile = (rows, LANES)
    tile_row = lax.broadcasted_iota(jnp.int32, tile, 0)
    tile_lane = lax.broadcasted_iota(jnp.int32, tile, 1)
    across_place = jnp.full(tile, -1, jnp.int32)
    down_place = jnp.zeros(tile, jnp.int32)
    for i in range(rows):
        across_place = jnp.where(tile_lane == i, places[i], across_place)
        down_place = jnp.where(tile_row == i, places[i], down_place)

    def anchor_rows(c):
        at = tile_lane + c * LANES - (me * pair_rows + rows)
        return jnp.where(at == down_place, -1.0, 0.0)

    early = bias_of(0) if chunks == 1 else None
    exchange.wait()

    def weigh(c):
        bias = early if chunks == 1 else bias_of(c)
        logits = (scores[part(c), :] + landed[part(c), :]) * inverse_temperature
        logits = logits.reshape(per_chunk, pair_rows, total)
        is_positive = column == own_column + c * LANES
        query_logits = jnp.where(is_document, logits[:, :rows] + bias, -jnp.inf)
        doc_logits = jnp.where(
            is_document & jnp.logical_not(is_positive), logits[:, rows:], -jnp.inf
        )
        peak = jnp.max(jnp.maximum(query_logits, doc_logits), axis=2, keepdims=True)
        query_terms, doc_terms = jnp.exp(query_logits - peak), jnp.exp(doc_logits - peak)
        mass = jnp.sum(query_terms + doc_terms, axis=2, keepdims=True)
        lse = peak + jnp.log(mass)
        share = 1.0 / mass
        losses = lse - jnp.sum(jnp.where(is_positive, query_logits, 0.0), axis=2, keepdims=True)
        weights = jnp.concatenate(
            [query_terms * share, doc_terms * share], axis=1
        )
        scores[part(c), :] = weights.reshape(LANES, total)
        landed[part(c), :LANES] = jnp.broadcast_to(
            jnp.concatenate([losses, losses], axis=1), (per_chunk, pair_rows, LANES)
        ).reshape(LANES, LANES)

    repeat(chunks, weigh)

    upper = pl.ds(pl.multiple_of(me * pair_rows, rows), rows)
    lower = pl.ds(pl.multiple_of(me * pair_rows + rows, rows), rows)
    sublane = lax.broadcasted_iota(jnp.int32, (rows, total), 0)
    heads = jnp.where(lane == me * pair_rows + sublane, -1.0, scores[lower, :])
    left_ref[: 2 * rows, :] = jnp.concatenate(
        [to_queries(scores[upper, :]), heads], axis=0
    ).astype(jnp.bfloat16)
    own_tile = pl.ds(pl.multiple_of(me // per_chunk * LANES, LANES), LANES)
    own_rows = pl.ds(
        pl.multiple_of(lax.rem(me, per_chunk) * pair_rows + rows, rows), rows
    )

    def columns(c):
        flipped[...] = scores[part(c), own_tile].T
        left_ref[2 * rows :, part(c)] = jnp.concatenate(
            [flipped[own_rows, :], anchor_rows(c)], axis=0
        ).astype(jnp.bfloat16)

    repeat(chunks, columns)

    losses = landed[upper, :LANES]
    at = lax.broadcasted_iota(jnp.int32, losses.shape, 0)
    loss_ref[...] = jnp.sum(jnp.where(across_place == at, losses, 0.0), axis=0, keepdims=True)

    block_copy(me, twin, 0).wait_send()
    repeat(depth - 1, lambda step: block_copy(me, twin, 1 + step).wait_send())
    repeat(depth - 1, lambda step: block_copy(me, twin, depth + step).wait_send())


def finish(width, left_ref, table_ref, loss_in, req_hbm, pas_hbm, loss_hbm, req, pas, loss, sem):
    rows = req.shape[0]
    loss[...] = loss_in[:, :rows]
    loss_copy = pltpu.make_async_copy(loss, loss_hbm, sem.at[2 * PIECES])
    loss_copy.start()
    total = left_ref.shape[1]
    step = width // PIECES
    copies = [loss_copy]
    for piece in range(PIECES):
        across = pl.ds(piece * step, step)
        out = jnp.zeros((4 * rows, step), jnp.float32)
        for start in range(0, total, LANES):
            depth = min(total, LANES)
            out = out + jnp.dot(
                left_ref[:, start : start + depth],
                table_ref[start : start + depth, across],
                preferred_element_type=jnp.float32,
            )
        req[:, across] = (out[:rows] + out[3 * rows :]) * inverse_temperature
        pas[:, across] = (out[rows : 2 * rows] + out[2 * rows : 3 * rows]) * inverse_temperature
        for which, (src, dst) in enumerate(((req, req_hbm), (pas, pas_hbm))):
            copy = pltpu.make_async_copy(
                src.at[:, across], dst.at[:, across], sem.at[2 * piece + which]
            )
            copy.start()
            copies.append(copy)
    for copy in copies:
        copy.wait()


def on_device(queries, documents, positive, hard_ids):
    n = lax.axis_size("row")
    rows, width = queries.shape
    total = 2 * rows * n
    vmem = pl.BlockSpec(memory_space=pltpu.VMEM)
    anywhere = pl.BlockSpec(memory_space=pl.ANY)
    inputs = (queries, documents, positive, hard_ids)
    table, left, losses = pl.pallas_call(
        functools.partial(kernel, n),
        out_shape=(
            pltpu.VMEM((total, width + total), jnp.bfloat16),
            pltpu.VMEM((4 * rows, total), jnp.bfloat16),
            pltpu.VMEM((1, LANES), jnp.float32),
        ),
        in_specs=[anywhere] * 4,
        out_specs=(vmem, vmem, vmem),
        scratch_shapes=[
            pltpu.VMEM((rows, width), jnp.float32),
            pltpu.VMEM((rows, width), jnp.float32),
            pltpu.SMEM((rows,), jnp.int32),
            pltpu.VMEM(hard_ids.shape, jnp.int32),
            pltpu.VMEM((total, total), jnp.float32),
            pltpu.VMEM((total, total), jnp.float32),
            pltpu.VMEM((LANES, LANES), jnp.float32),
            pltpu.SemaphoreType.DMA((4,)),
            pltpu.SemaphoreType.DMA((n - 1,)),
            pltpu.SemaphoreType.DMA((n,)),
            pltpu.SemaphoreType.DMA((2,)),
        ],
        compiler_params=pltpu.CompilerParams(
            collective_id=0,
            has_side_effects=True,
            vmem_limit_bytes=8 * total * total + 6 * 1024 * 1024,
        ),
    )(*(pltpu.with_memory_space_constraint(a, pltpu.HBM) for a in inputs))
    table, left, losses = (
        pltpu.with_memory_space_constraint(a, pltpu.VMEM) for a in (table, left, losses)
    )
    request, passage, losses = pl.pallas_call(
        functools.partial(finish, width),
        out_shape=(
            jax.ShapeDtypeStruct((rows, width), jnp.float32),
            jax.ShapeDtypeStruct((rows, width), jnp.float32),
            jax.ShapeDtypeStruct((1, rows), jnp.float32),
        ),
        in_specs=[vmem] * 3,
        out_specs=(anywhere,) * 3,
        scratch_shapes=[
            pltpu.VMEM((rows, width), jnp.float32),
            pltpu.VMEM((rows, width), jnp.float32),
            pltpu.VMEM((1, rows), jnp.float32),
            pltpu.SemaphoreType.DMA((2 * PIECES + 1,)),
        ],
        compiler_params=pltpu.CompilerParams(vmem_limit_bytes=6 * 1024 * 1024),
    )(left, table, losses)
    return request, passage, losses.reshape(rows)


def solution(mesh):
    return jax.shard_map(
        on_device,
        mesh=mesh,
        in_specs=(
            P(("groups", "row"), "col"),
            P(("groups", "row"), "col"),
            P(("groups", "row")),
            P(("groups", "row"), None),
        ),
        out_specs=(P(("groups", "row"), "col"), P(("groups", "row"), "col"), P(("groups", "row"))),
        check_vma=False,
    )
```
